128 devices in a mesh: row: 8 (over x_hi, y), col: 8 (over z, core), sec: 2 (over x_lo).
Axes of the slice: x: 4 (x_hi: 2, x_lo: 2; x = x_hi * 2 + x_lo), y: 4, z: 4, core: 2. Of those that a mesh axis runs over, the one named last changes fastest.
Arguments:
- centers: float32 [3, 4096], replicated, may hold values from 0 to 4
- charge_sites: float32 [3, 65536], P(None, ('row', 'col', 'sec')), may hold values from 0 to 4
- charges: float32 [65536], P(('row', 'col', 'sec')), may hold values from -0.25 to 0.25
- amplitudes: float32 [6], replicated, may hold values from 0.05 to 0.3
- widths: float32 [6], replicated, may hold values from 0.2 to 0.5
- core_matrix: float32 [4096, 4096], P('row', ('col', 'sec')), may hold values from -0.9 to 0.9, as said below
- pattern: int32 [64, 64], P('row', ('col', 'sec')), may hold values from 0 to 1, as said below
Outputs:
- sign_matrix: float32 [4096, 4096], P('row', ('col', 'sec'))
The draws below stay inside these ranges and needn't reach their ends.
Inputs may be any that keep to these rules, and one draw needn't show every extreme that they name: `pattern`: Symmetric; every diagonal block is 1. `core_matrix`: Symmetric, and zero outside the blocks that pattern marks.
All inputs are finite; a program needn't handle non-finite values.
Results may differ from the reference program's by a relative error of at most 0.0003.
Values sent between devices are 32-bit elements; how exact they have to be, the bound alone decides.
A program may use at most 64 MiB of HBM per device.

```python
import math
import jax
import jax.numpy as jnp
from jax import lax

BLOCK = 64
GAUSS = 6
STEPS = 2
NBLK = 64
NBF = 4096
NMM = 65536


def block_pattern(key):
    pick_values = jax.random.randint(key, (NBLK, NBLK), 0, 4)
    rows_id = lax.broadcasted_iota(jnp.int32, (NBLK, NBLK), 0)
    cols_id = lax.broadcasted_iota(jnp.int32, (NBLK, NBLK), 1)
    upper = (pick_values == 0) & (rows_id < cols_id)
    return jnp.where(upper | upper.T | (rows_id == cols_id), 1, 0).astype(jnp.int32)


def draw_pattern(key, part):
    return block_pattern(key)


def draw_core_matrix(key, part):
    shared = block_pattern(key)
    key = jax.random.fold_in(key, 7)
    noise_key, diag_key = jax.random.split(key, 2)
    element = jnp.repeat(jnp.repeat(shared, BLOCK, axis=0), BLOCK, axis=1)
    raw_values = 0.0127 * jax.random.truncated_normal(noise_key, -6.0, 6.0, (NBF, NBF), jnp.float32)
    diagonal = jax.random.uniform(diag_key, (NBF,), jnp.float32, -0.9, 0.9)
    off_values = 0.5 * (raw_values + raw_values.T)
    rows_id = lax.broadcasted_iota(jnp.int32, (NBF, NBF), 0)
    cols_id = lax.broadcasted_iota(jnp.int32, (NBF, NBF), 1)
    return jnp.where(rows_id == cols_id, diagonal[:, None], jnp.where(element == 1, off_values, 0.0))


def levels(rng, shape, cuts, smallest, top_value):
    level, own = 1.0, jax.random.fold_in(rng, 6)
    for axis_at, blocks in cuts:
        heights = jnp.exp(jax.random.uniform(jax.random.fold_in(own, axis_at), (blocks,), jnp.float32, smallest / len(cuts), top_value / len(cuts)))
        level = level * jnp.repeat(heights, shape[axis_at] // blocks).reshape([-1 if axis == axis_at else 1 for axis in range(len(shape))])
    return level


def noise(key, extent, deviation, most, shards=(), held_as=jnp.bfloat16):
    level = levels(key, extent, shards, -0.22, 0.18) if shards else 1.0
    values = jax.random.normal(key, extent, jnp.float32) * deviation * level
    return jnp.minimum(jnp.maximum(values, -most), most).astype(held_as)


def setup_inputs(seed: int = 0) -> dict:
    seeds = jax.random.split(jax.random.key(seed), 8)
    return {
        "centers": jnp.clip(jax.random.uniform(seeds[0], (3, NBF), jnp.float32, 0.0, 4.0), 0.0, 4.0),
        "charge_sites": jnp.clip(4.0 * jax.random.uniform(seeds[1], (3, NMM), jnp.float32) ** levels(seeds[1], (3, NMM), ((1, 128),), -0.2, 0.2), 0.0, 4.0),
        "charges": noise(seeds[2], (NMM,), (NMM // 128) ** -0.5, 0.25, ((0, 128),), jnp.float32),
        "amplitudes": jnp.clip(jnp.exp(jax.random.uniform(seeds[3], (GAUSS,), jnp.float32, math.log(0.05), math.log(0.3))), 0.05, 0.3),
        "widths": jnp.clip(jnp.exp(jax.random.uniform(seeds[4], (GAUSS,), jnp.float32, math.log(0.2), math.log(0.5))), 0.2, 0.5),
        "core_matrix": draw_core_matrix(jax.random.fold_in(seeds[7], 71), 0),
        "pattern": draw_pattern(jax.random.fold_in(seeds[7], 71), 0),
    }


def potential(centers, charge_sites, charges, amplitudes, widths):
    block_len = 256
    blocks = centers.reshape(3, NBF // block_len, block_len).transpose(1, 0, 2)
    inverse = 1.0 / (widths * widths)

    def one_block(points):
        distance = (points[0][:, None] - charge_sites[0][None, :]) ** 2
        distance = distance + (points[1][:, None] - charge_sites[1][None, :]) ** 2
        distance = distance + (points[2][:, None] - charge_sites[2][None, :]) ** 2
        kernel = amplitudes[0] * jnp.exp(-distance * inverse[0])
        for term_number in range(1, GAUSS):
            kernel = kernel + amplitudes[term_number] * jnp.exp(-distance * inverse[term_number])
        return jnp.dot(kernel, charges, precision=lax.Precision.HIGHEST, preferred_element_type=jnp.float32)

    return lax.map(one_block, blocks).reshape(NBF)


def reference(centers, charge_sites, charges, amplitudes, widths, core_matrix, pattern):
    field = potential(centers, charge_sites, charges, amplitudes, widths)
    element_mask = jnp.repeat(jnp.repeat(pattern, BLOCK, axis=0), BLOCK, axis=1).astype(jnp.float32)
    current = core_matrix + jnp.diag(field)
    for iteration in range(STEPS):
        square = element_mask * jnp.dot(current, current, precision=lax.Precision.HIGHEST, preferred_element_type=jnp.float32)
        current = element_mask * (1.5 * current - 0.5 * jnp.dot(square, current, precision=lax.Precision.HIGHEST, preferred_element_type=jnp.float32))
    return current
```

```python
import functools

import jax
import jax.numpy as jnp
from jax import lax
from jax.experimental import pallas as pl
from jax.experimental.pallas import tpu as pltpu
from jax.sharding import PartitionSpec as P

BLOCK = 64
STEPS = 2
ROWS, COLS, SECS = 8, 8, 2
TILES = COLS * SECS
CAP = 20
PAIRS = CAP // 2
HALF = PAIRS // 2
CHUNK = 128
LOG2E = 1.4426950408889634
MESH = pl.DeviceIdType.MESH
AXES = ("row", "col", "sec")


def local_field(centers, charge_sites, charges, amplitudes, widths):
    center_count = centers.shape[1]
    block_len = min(512, center_count)
    blocks = centers.reshape(3, center_count // block_len, block_len).transpose(1, 0, 2)
    inverse = 1.0 / (widths * widths)

    def one_block(points):
        distance = (points[0][:, None] - charge_sites[0][None, :]) ** 2
        distance = distance + (points[1][:, None] - charge_sites[1][None, :]) ** 2
        distance = distance + (points[2][:, None] - charge_sites[2][None, :]) ** 2
        kernel = amplitudes[0] * jnp.exp(-distance * inverse[0])
        for term_number in range(1, amplitudes.shape[0]):
            kernel = kernel + amplitudes[term_number] * jnp.exp(-distance * inverse[term_number])
        return jnp.dot(
            kernel, charges, precision=lax.Precision.HIGHEST, preferred_element_type=jnp.float32
        )

    return lax.map(one_block, blocks).reshape(center_count)


def diagonal_piece(values, row_first, col_first, row_count, col_count):
    rows_id = row_first + lax.broadcasted_iota(jnp.int32, (row_count, col_count), 0)
    cols_id = col_first + lax.broadcasted_iota(jnp.int32, (row_count, col_count), 1)
    return jnp.where(rows_id == cols_id, values[:, None], 0.0)


def column_panel(block_tile):
    return lax.all_gather(block_tile, "row", axis=0, tiled=True)


def fold_rows(block_tile, col_panel):
    return jnp.dot(
        lax.all_gather(block_tile, ("col", "sec"), axis=1, tiled=True),
        col_panel,
        precision=lax.Precision.HIGHEST,
        preferred_element_type=jnp.float32,
    )


def dense_body(centers, charge_sites, charges, amplitudes, widths, core_matrix, pattern):
    row_count, col_count = core_matrix.shape
    row_first = lax.axis_index("row") * row_count
    col_first = lax.axis_index(("col", "sec")) * col_count
    element_mask = jnp.repeat(jnp.repeat(pattern, BLOCK, axis=0), BLOCK, axis=1).astype(jnp.float32)
    field = lax.psum(local_field(centers, charge_sites, charges, amplitudes, widths), AXES)
    row_field = lax.dynamic_slice_in_dim(field, row_first, row_count, 0)
    current = core_matrix + diagonal_piece(row_field, row_first, col_first, row_count, col_count)
    for _ in range(STEPS):
        right_panel = column_panel(current)
        square = element_mask * fold_rows(current, right_panel)
        current = element_mask * (1.5 * current - 0.5 * fold_rows(square, right_panel))
    return current


def kernel(
    inv_ref,
    keep_ref,
    coef_ref,
    hdr_ref,
    centers_ref,
    sites_ref,
    charges_ref,
    core_ref,
    out_ref,
    flag_ref,
    rbuf,
    cbuf,
    a_hi,
    a_lo,
    b_hi,
    b_lo,
    acc,
    work,
    cur,
    sq,
    fan,
    f_own,
    f_one,
    f_two,
    f_three,
    f_sum,
    f_all,
    fi_col,
    hrow,
    hcol,
    trow,
    tcol,
    r_send,
    r_recv,
    c_send,
    c_recv,
    hr_send,
    hr_recv,
    hc_send,
    hc_recv,
    f1_send,
    f1_recv,
    f2_send,
    f2_recv,
    f3_send,
    f3_recv,
    t_sem,
):
    row, col, sec = lax.axis_index("row"), lax.axis_index("col"), lax.axis_index("sec")
    hi, y = row // 4, row % 4
    z, core = col // 2, col % 2
    me = 2 * col + sec

    sibling = (row, 2 * z + (1 - core), sec)
    x_peer = (row, col, 1 - sec)
    z_up = (row, 2 * ((z + 1) % 4) + core, sec)
    z_down = (row, 2 * ((z + 3) % 4) + core, sec)
    h_peer = ((row + 4) % 8, col, sec)
    y_up = (4 * hi + (y + 1) % 4, col, sec)
    y_down = (4 * hi + (y + 3) % 4, col, sec)

    def row_mate(d):
        other = (me + d) % TILES
        return (row, other // 2, other % 2)

    def col_mate(d):
        return ((row + d) % ROWS, col, sec)

    lane = lax.broadcasted_iota(jnp.int32, (BLOCK, 128), 1)
    sub = lax.broadcasted_iota(jnp.int32, (BLOCK, 128), 0)
    left = lane < BLOCK

    barrier = pltpu.get_barrier_semaphore()

    def greet_row(d, c):
        pl.semaphore_signal(barrier, inc=1, device_id=row_mate(d), device_id_type=MESH)
        return c

    def greet_col(d, c):
        pl.semaphore_signal(barrier, inc=1, device_id=col_mate(d), device_id_type=MESH)
        return c

    lax.fori_loop(1, TILES, greet_row, 0)
    lax.fori_loop(1, ROWS, greet_col, 0)


    def put(dst, number, value):
        dst[number] = value
        dst[16 + number] = pltpu.roll(value, BLOCK, 1)

    def compact(src, store):
        for u in range(PAIRS):
            value = jnp.where(left, src[inv_ref[0, 2 * u]], src[inv_ref[0, 2 * u + 1]])
            store(u, value)

    def unpack(load, table, tile, store):
        for u in range(PAIRS):
            value = load(u)
            work[u] = value
            work[PAIRS + 1 + u] = pltpu.roll(value, BLOCK, 1)
        for b in range(16):
            value = jnp.where(
                left, work[table[tile, 0, 2 * b]], work[table[tile, 0, 2 * b + 1]]
            )
            high = value.astype(jnp.bfloat16)
            low = (value - high.astype(jnp.float32)).astype(jnp.bfloat16)
            store(b, high, low)

    def unpack_row(p, tile):
        def store(b, high, low):
            at = (tile, pl.ds((b // 2) * BLOCK, BLOCK), pl.ds((b % 2) * 128, 128))
            a_hi[at] = high
            a_lo[at] = low

        unpack(lambda u: rbuf[p, tile, u], trow, tile, store)

    def unpack_col(step, tile):
        def store(b, high, low):
            at = (
                2 * tile + b // 8,
                pl.ds((b // 2 % 4) * BLOCK, BLOCK),
                pl.ds((b % 2) * 128, 128),
            )
            b_hi[at] = high
            b_lo[at] = low

        unpack(lambda u: cbuf[step, tile, u], tcol, tile, store)

    def fold(tile):
        dot = functools.partial(jnp.dot, preferred_element_type=jnp.float32)
        total = dot(a_hi[tile], b_hi[tile])
        total = total + dot(a_lo[tile], b_hi[tile])
        total = total + dot(a_hi[tile], b_lo[tile])
        acc[...] += total


    def halves(p, j):
        return [pl.ds(0, HALF), pl.ds(HALF, HALF)]

    def row_copy(p, tile, j, kind, h, dev):
        ref = rbuf.at[p, tile, pl.ds(h * HALF, HALF)]
        return pltpu.make_async_remote_copy(
            src_ref=ref,
            dst_ref=ref,
            send_sem=r_send.at[j, kind, h],
            recv_sem=r_recv.at[p, tile, h],
            device_id=dev,
            device_id_type=MESH,
        )

    def col_copy(s, tile, j, kind, h, dev):
        ref = cbuf.at[s, tile, pl.ds(h * HALF, HALF)]
        return pltpu.make_async_remote_copy(
            src_ref=ref,
            dst_ref=ref,
            send_sem=c_send.at[j, kind, h],
            recv_sem=c_recv.at[s, tile, h],
            device_id=dev,
            device_id_type=MESH,
        )

    def offset(k):
        return 3 * k - 5 * (k // 2) - 2 * (k // 3)

    def row_tile(j):
        return 4 * ((z + offset(j // 2)) % 4) + 2 * core + (sec + j) % 2

    def peer_tile(j):
        return 4 * ((z + offset(j // 2)) % 4) + 2 * (1 - core) + (sec + j) % 2

    def col_tile(j):
        return 4 * ((hi + j) % 2) + (y + offset(j // 2)) % 4

    def row_out(p, j, act):
        tile = row_tile(j)

        @pl.when(j < 2)
        def _():
            for h in range(2):
                act(row_copy(p, tile, j, 1, h, z_up))
                act(row_copy(p, tile, j, 2, h, z_down))

        @pl.when(j == 0)
        def _():
            for h in range(2):
                act(row_copy(p, tile, j, 3, h, x_peer))

        @pl.when(j // 2 == 1)
        def _():
            act(row_copy(p, tile, j, 1, 0, z_up))

        @pl.when(j // 2 == 2)
        def _():
            act(row_copy(p, tile, j, 2, 1, z_down))

        for h in range(2):
            act(row_copy(p, tile, j, 0, h, sibling))

    def col_out(s, j, act):
        tile = col_tile(j)

        @pl.when(j == 0)
        def _():
            for h in range(2):
                act(col_copy(s, tile, j, 2, h, h_peer))

        @pl.when(j < 2)
        def _():
            for h in range(2):
                act(col_copy(s, tile, j, 0, h, y_up))
                act(col_copy(s, tile, j, 1, h, y_down))

        @pl.when(j // 2 == 1)
        def _():
            act(col_copy(s, tile, j, 0, 0, y_up))

        @pl.when(j // 2 == 2)
        def _():
            act(col_copy(s, tile, j, 1, 1, y_down))

    def start(copy):
        copy.start()

    def drain(copy):
        copy.wait_send()

    def row_in(p, tile):
        for h in range(2):
            row_copy(p, tile, 0, 0, h, sibling).wait_recv()

    def col_in(s, tile):
        for h in range(2):
            col_copy(s, tile, 0, 0, h, y_up).wait_recv()

    def row_drain(p):
        def one(j, c):
            row_out(p, j, drain)
            return c

        lax.fori_loop(0, 8, one, 0)

    def col_drain(s):
        def one(j, c):
            col_out(s, j, drain)
            return c

        lax.fori_loop(0, 6, one, 0)

    def small(src, dst, send, recv, dev):
        return pltpu.make_async_remote_copy(
            src_ref=src, dst_ref=dst, send_sem=send, recv_sem=recv,
            device_id=dev, device_id_type=MESH,
        )

    def loop(first, last, f):
        def one(d, c):
            f(d)
            return c

        lax.fori_loop(first, last, one, 0)


    for b in range(16):
        put(cur, b, core_ref[pl.ds((b // 2) * BLOCK, BLOCK), pl.ds((b % 2) * 128, 128)])

    def keep_iterate(p, s):
        def store(u, value):
            rbuf[p, me, u] = value
            cbuf[s, row, u] = value

        compact(cur, store)

    keep_iterate(0, 0)
    work[PAIRS] = jnp.zeros((BLOCK, 128), jnp.float32)
    work[2 * PAIRS + 1] = jnp.zeros((BLOCK, 128), jnp.float32)
    hrow[me] = hdr_ref[...]
    hcol[row] = hdr_ref[...]

    pl.semaphore_wait(barrier, TILES - 1 + ROWS - 1)

    def hr_copy(d):
        return small(hdr_ref, hrow.at[me], hr_send.at[d], hr_recv.at[me], row_mate(d))

    def hc_copy(d):
        return small(hdr_ref, hcol.at[row], hc_send.at[d], hc_recv.at[row], col_mate(d))

    loop(1, TILES, lambda d: hr_copy(d).start())
    loop(1, ROWS, lambda d: hc_copy(d).start())

    def read_tables():
        def wait_row(d):
            other = (me + d) % TILES
            small(hdr_ref, hrow.at[other], hr_send.at[d], hr_recv.at[other], row_mate(d)).wait_recv()

        def wait_col(d):
            other = (row + d) % ROWS
            small(hdr_ref, hcol.at[other], hc_send.at[d], hc_recv.at[other], col_mate(d)).wait_recv()

        loop(1, TILES, wait_row)
        loop(1, ROWS, wait_col)
        one = pltpu.make_async_copy(hrow, trow, t_sem.at[0])
        two = pltpu.make_async_copy(hcol, tcol, t_sem.at[1])
        one.start()
        two.start()
        one.wait()
        two.wait()


    def spread_sites():
        for a in range(4):
            for c in range(4):
                if a < 3:
                    line = sites_ref[a : a + 1, c * 128 : (c + 1) * 128]
                else:
                    line = charges_ref[0:1, c * 128 : (c + 1) * 128]
                fan[a, c * 128 : (c + 1) * 128, :] = jnp.transpose(
                    jnp.broadcast_to(line, (128, 128))
                )

    def field_chunk(ch):
        at = pl.ds(pl.multiple_of(ch * CHUNK, CHUNK), CHUNK)
        px = centers_ref[0:1, at]
        py = centers_ref[1:2, at]
        pz = centers_ref[2:3, at]

        def some(m, total):
            part = pl.ds(m * 32, 32)
            dx = fan[0, part, :] - px
            dy = fan[1, part, :] - py
            dz = fan[2, part, :] - pz
            distance = dx * dx + dy * dy + dz * dz
            value = coef_ref[1, 0] * jnp.exp2(distance * coef_ref[0, 0])
            for g in range(1, 6):
                value = value + coef_ref[1, g] * jnp.exp2(distance * coef_ref[0, g])
            return total + value * fan[3, part, :]

        total = lax.fori_loop(0, 16, some, jnp.zeros((32, 128), jnp.float32), unroll=4)
        f_own[ch // 4, pl.ds(ch % 4, 1), :] = jnp.sum(total, axis=0, keepdims=True)

    def f1_copy(d):
        other = (row + d) % ROWS
        return small(f_own.at[other], f_one.at[row], f1_send.at[d], f1_recv.at[row], col_mate(d))

    def f1_wait(d):
        other = (row + d) % ROWS
        small(f_own.at[row], f_one.at[other], f1_send.at[d], f1_recv.at[other], col_mate(d)).wait_recv()

    def f2_copy(d):
        return small(f_sum, f_two.at[me], f2_send.at[d], f2_recv.at[me], row_mate(d))

    def f2_wait(d):
        other = (me + d) % TILES
        small(f_sum, f_two.at[other], f2_send.at[d], f2_recv.at[other], row_mate(d)).wait_recv()

    def f3_copy(d):
        return small(f_all, f_three.at[row], f3_send.at[d], f3_recv.at[row], col_mate(d))

    def f3_wait(d):
        other = (row + d) % ROWS
        small(f_all, f_three.at[other], f3_send.at[d], f3_recv.at[other], col_mate(d)).wait_recv()

    line8 = lax.broadcasted_iota(jnp.int32, (8, 128), 0)

    def field_first():
        f_one[row] = f_own[row]
        loop(1, ROWS, lambda d: f1_copy(d).start())

    def field_second():
        loop(1, ROWS, f1_wait)
        total = f_one[0]
        for r in range(1, ROWS):
            total = total + f_one[r]
        count = jnp.broadcast_to(hdr_ref[1:2, :], (8, 128)).astype(jnp.float32)
        total = jnp.where(line8 < 4, total, count)
        f_sum[...] = total
        f_two[me] = total
        loop(1, TILES, lambda d: f2_copy(d).start())

    def field_third():
        loop(1, TILES, f2_wait)
        total = f_two[0]
        most = f_two[0]
        for c in range(1, TILES):
            value = f_two[c]
            total = total + value
            most = jnp.maximum(most, value)
        total = jnp.where(line8 < 4, total, most)
        f_all[...] = total
        f_three[row] = total
        loop(1, ROWS, lambda d: f3_copy(d).start())

    def field_last():
        loop(1, ROWS, f3_wait)
        most = f_three[0]
        for r in range(1, ROWS):
            most = jnp.maximum(most, f_three[r])
        flag_ref[...] = most
        for c in range(4):
            line = f_three[row, c : c + 1, :]
            fi_col[c * 128 : (c + 1) * 128, :] = jnp.transpose(jnp.broadcast_to(line, (128, 128)))
        loop(1, ROWS, lambda d: f1_copy(d).wait_send())
        loop(1, TILES, lambda d: f2_copy(d).wait_send())
        loop(1, ROWS, lambda d: f3_copy(d).wait_send())
        loop(1, TILES, lambda d: hr_copy(d).wait_send())
        loop(1, ROWS, lambda d: hc_copy(d).wait_send())


    def one_step(step, carry):
        p = 2 * step
        first = step == 0

        def arrive(j):
            @pl.when(j > 0)
            def _():
                row_in(p, row_tile(j))

            row_out(p, j, start)

            @pl.when(j > 0)
            def _():
                col_in(step, col_tile(j))

            col_out(step, j, start)

            @pl.when(first)
            def _():
                @pl.when(j == 0)
                def _():
                    spread_sites()

                loop(4 * j, 4 * j + 4, field_chunk)

                @pl.when(j == 0)
                def _():
                    read_tables()

            unpack_row(p, row_tile(j))
            unpack_col(step, col_tile(j))

        loop(0, 8, arrive)

        @pl.when(first)
        def _():
            field_first()

        acc[...] = jnp.zeros_like(acc)

        def from_peer(j):
            fold(row_tile(j))

            @pl.when(first)
            def _():
                @pl.when(j == 2)
                def _():
                    field_second()

                @pl.when(j == 5)
                def _():
                    field_third()

            row_in(p, peer_tile(j))
            unpack_row(p, peer_tile(j))
            fold(peer_tile(j))

        loop(0, 8, from_peer)

        @pl.when(first)
        def _():
            field_last()

        scale = jnp.where(first, 1.0, 0.0)

        def pieces(b):
            at = (pl.ds((b // 2) * BLOCK, BLOCK), pl.ds((b % 2) * 128, 128))
            fi = scale * fi_col[pl.ds((b // 2) * BLOCK, BLOCK), :]
            fj = scale * f_three[me // 2, pl.ds((me % 2) * 2 + b % 2, 1), :]
            same = (sub + (512 * row + (b // 2) * BLOCK)) == (lane + (256 * me + (b % 2) * 128))
            return at, fi, fj, same

        for b in range(16):
            at, fi, fj, same = pieces(b)
            value = acc[at] + (fi + fj) * cur[b] + jnp.where(same, fi * fi, 0.0)
            put(sq, b, value)

        def store(u, value):
            rbuf[p + 1, me, u] = value

        compact(sq, store)
        row_drain(p)

        acc[...] = jnp.zeros_like(acc)

        def arrive_square(j):
            @pl.when(j > 0)
            def _():
                row_in(p + 1, row_tile(j))

            row_out(p + 1, j, start)
            unpack_row(p + 1, row_tile(j))
            fold(row_tile(j))

        loop(0, 8, arrive_square)

        def from_peer_square(j):
            row_in(p + 1, peer_tile(j))
            unpack_row(p + 1, peer_tile(j))
            fold(peer_tile(j))

        loop(0, 8, from_peer_square)

        for b in range(16):
            at, fi, fj, same = pieces(b)
            value = 1.5 * (cur[b] + jnp.where(same, fi, 0.0)) - 0.5 * (acc[at] + sq[b] * fj)
            put(cur, b, value)

        row_drain(p + 1)
        col_drain(step)

        @pl.when(step + 1 < STEPS)
        def _():
            keep_iterate(p + 2, step + 1)

        return carry

    lax.fori_loop(0, STEPS, one_step, 0)

    for b in range(16):
        at = (pl.ds((b // 2) * BLOCK, BLOCK), pl.ds((b % 2) * 128, 128))
        keep_left = keep_ref[b // 2, 2 * (b % 2)].astype(jnp.float32)
        keep_right = keep_ref[b // 2, 2 * (b % 2) + 1].astype(jnp.float32)
        out_ref[at] = cur[b] * jnp.where(left, keep_left, keep_right)


def tables(pattern):
    keep = pattern.reshape(32)
    number = lax.broadcasted_iota(jnp.int32, (32, 32), 0)
    other = lax.broadcasted_iota(jnp.int32, (32, 32), 1)
    before = jnp.sum(jnp.where(other < number, keep[None, :], 0), axis=1)
    block = lax.iota(jnp.int32, 32)
    turned = (before + block) % 2
    code = jnp.where((keep == 1) & (before < CAP), before // 2 + (PAIRS + 1) * turned, PAIRS)
    slot = lax.iota(jnp.int32, CAP)
    source = block[None, :] // 2 + 16 * ((block[None, :] + slot[:, None]) % 2)
    inverse = jnp.sum(
        jnp.where((keep[None, :] == 1) & (before[None, :] == slot[:, None]), source, 0), axis=1
    )
    header = jnp.zeros((8, 128), jnp.int32).at[0, :32].set(code)
    header = header.at[1, :].set(jnp.sum(keep))
    return header, inverse[None, :]


def body(centers, charge_sites, charges, amplitudes, widths, core_matrix, pattern):
    header, inverse = tables(pattern)
    coef = jnp.stack([-LOG2E / (widths * widths), amplitudes])
    vmem = pl.BlockSpec(memory_space=pltpu.VMEM)
    smem = pl.BlockSpec(memory_space=pltpu.SMEM)
    f32, bf16 = jnp.float32, jnp.bfloat16
    dma = pltpu.SemaphoreType.DMA
    out, flag = pl.pallas_call(
        kernel,
        out_shape=(
            jax.ShapeDtypeStruct((512, 256), f32),
            jax.ShapeDtypeStruct((8, 128), f32),
        ),
        in_specs=[smem, smem, smem, vmem, vmem, vmem, vmem, vmem],
        out_specs=(vmem, vmem),
        scratch_shapes=[
            pltpu.VMEM((4, TILES, PAIRS, BLOCK, 128), f32),
            pltpu.VMEM((2, ROWS, PAIRS, BLOCK, 128), f32),
            pltpu.VMEM((TILES, 512, 256), bf16),
            pltpu.VMEM((TILES, 512, 256), bf16),
            pltpu.VMEM((TILES, 256, 256), bf16),
            pltpu.VMEM((TILES, 256, 256), bf16),
            pltpu.VMEM((512, 256), f32),
            pltpu.VMEM((2 * PAIRS + 2, BLOCK, 128), f32),
            pltpu.VMEM((32, BLOCK, 128), f32),
            pltpu.VMEM((32, BLOCK, 128), f32),
            pltpu.VMEM((4, 512, 128), f32),
            pltpu.VMEM((ROWS, 8, 128), f32),
            pltpu.VMEM((ROWS, 8, 128), f32),
            pltpu.VMEM((TILES, 8, 128), f32),
            pltpu.VMEM((ROWS, 8, 128), f32),
            pltpu.VMEM((8, 128), f32),
            pltpu.VMEM((8, 128), f32),
            pltpu.VMEM((512, 128), f32),
            pltpu.VMEM((TILES, 8, 128), jnp.int32),
            pltpu.VMEM((ROWS, 8, 128), jnp.int32),
            pltpu.SMEM((TILES, 8, 128), jnp.int32),
            pltpu.SMEM((ROWS, 8, 128), jnp.int32),
            dma((8, 4, 2)),
            dma((4, TILES, 2)),
            dma((8, 3, 2)),
            dma((2, ROWS, 2)),
            dma((TILES,)),
            dma((TILES,)),
            dma((ROWS,)),
            dma((ROWS,)),
            dma((ROWS,)),
            dma((ROWS,)),
            dma((TILES,)),
            dma((TILES,)),
            dma((ROWS,)),
            dma((ROWS,)),
            dma((2,)),
        ],
        compiler_params=pltpu.CompilerParams(
            collective_id=0, has_side_effects=True, vmem_limit_bytes=58 * 1024 * 1024
        ),
    )(
        inverse,
        pattern,
        coef,
        header,
        centers,
        charge_sites,
        charges[None, :],
        core_matrix,
    )
    return lax.cond(
        flag[4, 0] > CAP,
        lambda: dense_body(
            centers, charge_sites, charges, amplitudes, widths, core_matrix, pattern
        ),
        lambda: out,
    )


def solution(mesh):
    return jax.shard_map(
        body,
        mesh=mesh,
        in_specs=(
            P(),
            P(None, AXES),
            P(AXES),
            P(),
            P(),
            P("row", ("col", "sec")),
            P("row", ("col", "sec")),
        ),
        out_specs=P("row", ("col", "sec")),
        check_vma=False,
    )
```

```python
import functools

import jax
import jax.numpy as jnp
from jax import lax
from jax.experimental import pallas as pl
from jax.experimental.pallas import tpu as pltpu
from jax.sharding import PartitionSpec as P

BLOCK = 64
STEPS = 2
ROWS, COLS, SECS = 8, 8, 2
TILES = COLS * SECS
CAP = 20
PAIRS = CAP // 2
HALF = PAIRS // 2
CHUNK = 128
LOG2E = 1.4426950408889634
MESH = pl.DeviceIdType.MESH
AXES = ("row", "col", "sec")


def local_field(centers, charge_sites, charges, amplitudes, widths):
    center_count = centers.shape[1]
    block_len = min(512, center_count)
    blocks = centers.reshape(3, center_count // block_len, block_len).transpose(1, 0, 2)
    inverse = 1.0 / (widths * widths)

    def one_block(points):
        distance = (points[0][:, None] - charge_sites[0][None, :]) ** 2
        distance = distance + (points[1][:, None] - charge_sites[1][None, :]) ** 2
        distance = distance + (points[2][:, None] - charge_sites[2][None, :]) ** 2
        kernel = amplitudes[0] * jnp.exp(-distance * inverse[0])
        for term_number in range(1, amplitudes.shape[0]):
            kernel = kernel + amplitudes[term_number] * jnp.exp(-distance * inverse[term_number])
        return jnp.dot(
            kernel, charges, precision=lax.Precision.HIGHEST, preferred_element_type=jnp.float32
        )

    return lax.map(one_block, blocks).reshape(center_count)


def diagonal_piece(values, row_first, col_first, row_count, col_count):
    rows_id = row_first + lax.broadcasted_iota(jnp.int32, (row_count, col_count), 0)
    cols_id = col_first + lax.broadcasted_iota(jnp.int32, (row_count, col_count), 1)
    return jnp.where(rows_id == cols_id, values[:, None], 0.0)


def column_panel(block_tile):
    return lax.all_gather(block_tile, "row", axis=0, tiled=True)


def fold_rows(block_tile, col_panel):
    return jnp.dot(
        lax.all_gather(block_tile, ("col", "sec"), axis=1, tiled=True),
        col_panel,
        precision=lax.Precision.HIGHEST,
        preferred_element_type=jnp.float32,
    )


def dense_body(centers, charge_sites, charges, amplitudes, widths, core_matrix, pattern):
    row_count, col_count = core_matrix.shape
    row_first = lax.axis_index("row") * row_count
    col_first = lax.axis_index(("col", "sec")) * col_count
    element_mask = jnp.repeat(jnp.repeat(pattern, BLOCK, axis=0), BLOCK, axis=1).astype(jnp.float32)
    field = lax.psum(local_field(centers, charge_sites, charges, amplitudes, widths), AXES)
    row_field = lax.dynamic_slice_in_dim(field, row_first, row_count, 0)
    current = core_matrix + diagonal_piece(row_field, row_first, col_first, row_count, col_count)
    for _ in range(STEPS):
        right_panel = column_panel(current)
        square = element_mask * fold_rows(current, right_panel)
        current = element_mask * (1.5 * current - 0.5 * fold_rows(square, right_panel))
    return current


def kernel(
    keep_ref,
    amp_ref,
    width_ref,
    centers_ref,
    sites_ref,
    charges_ref,
    core_ref,
    out_ref,
    flag_ref,
    rbuf,
    cbuf,
    a_hi,
    a_lo,
    b_hi,
    b_lo,
    acc,
    work,
    cur,
    sq,
    fan,
    f_own,
    f_one,
    f_two,
    f_three,
    f_sum,
    f_all,
    fi_col,
    hdr_ref,
    inv_line,
    coef_line,
    hrow,
    hcol,
    inv_ref,
    coef_ref,
    trow,
    tcol,
    r_send,
    r_recv,
    c_send,
    c_recv,
    hr_send,
    hr_recv,
    hc_send,
    hc_recv,
    f1_send,
    f1_recv,
    f2_send,
    f2_recv,
    f3_send,
    f3_recv,
    t_sem,
):
    row, col, sec = lax.axis_index("row"), lax.axis_index("col"), lax.axis_index("sec")
    hi, y = row // 4, row % 4
    z, core = col // 2, col % 2
    me = 2 * col + sec

    sibling = (row, 2 * z + (1 - core), sec)
    x_peer = (row, col, 1 - sec)
    z_up = (row, 2 * ((z + 1) % 4) + core, sec)
    z_down = (row, 2 * ((z + 3) % 4) + core, sec)
    across = ((row + 4) % 8, col, 1 - sec)
    y_up = (4 * hi + (y + 1) % 4, col, sec)
    y_down = (4 * hi + (y + 3) % 4, col, sec)

    def row_mate(d):
        other = (me + d) % TILES
        return (row, other // 2, other % 2)

    def col_mate(d):
        return ((row + d) % ROWS, col, sec)

    lane = lax.broadcasted_iota(jnp.int32, (BLOCK, 128), 1)
    sub = lax.broadcasted_iota(jnp.int32, (BLOCK, 128), 0)
    left = lane < BLOCK

    barrier = pltpu.get_barrier_semaphore()

    def greet_row(d, c):
        pl.semaphore_signal(barrier, inc=1, device_id=row_mate(d), device_id_type=MESH)
        return c

    def greet_col(d, c):
        pl.semaphore_signal(barrier, inc=1, device_id=col_mate(d), device_id_type=MESH)
        return c

    lax.fori_loop(1, TILES, greet_row, 0)
    lax.fori_loop(1, ROWS, greet_col, 0)
    pl.semaphore_signal(barrier, inc=1, device_id=across, device_id_type=MESH)


    lane1 = lax.broadcasted_iota(jnp.int32, (1, 128), 1)
    before = 0
    codes = jnp.full((1, 128), PAIRS, jnp.int32)
    blocks = jnp.zeros((1, 128), jnp.int32)
    for b in range(32):
        keep = keep_ref[b // 4, b % 4]
        turned = (before + b) % 2
        there = before // 2 + (PAIRS + 1) * turned
        code = jnp.where((keep == 1) & (before < CAP), there, PAIRS)
        codes = jnp.where(lane1 == b, code, codes)
        at = jnp.where(keep == 1, before, 127)
        blocks = jnp.where(lane1 == at, b // 2 + 16 * turned, blocks)
        before = before + keep
    hdr_ref[...] = jnp.where(lane1 == 127, before, codes)
    inv_line[...] = jnp.where(lane1 < CAP, blocks, 0)
    scale_line = jnp.zeros((1, 128), jnp.float32)
    for g in range(6):
        wide = jnp.full((1, 128), width_ref[g], jnp.float32)
        scale_line = jnp.where(lane1 == g, -LOG2E / (wide * wide), scale_line)
    coef_line[...] = scale_line
    inv_copy = pltpu.make_async_copy(inv_line, inv_ref, t_sem.at[0])
    coef_copy = pltpu.make_async_copy(coef_line, coef_ref, t_sem.at[1])
    inv_copy.start()
    coef_copy.start()


    def put(dst, number, value):
        dst[number] = value
        dst[16 + number] = pltpu.roll(value, BLOCK, 1)

    def compact(src, store):
        for u in range(PAIRS):
            value = jnp.where(left, src[inv_ref[0, 2 * u]], src[inv_ref[0, 2 * u + 1]])
            store(u, value)

    def unpack(load, table, tile, store):
        for u in range(PAIRS):
            value = load(u)
            work[u] = value
            work[PAIRS + 1 + u] = pltpu.roll(value, BLOCK, 1)
        for b in range(16):
            value = jnp.where(
                left, work[table[tile, 0, 2 * b]], work[table[tile, 0, 2 * b + 1]]
            )
            high = value.astype(jnp.bfloat16)
            low = (value - high.astype(jnp.float32)).astype(jnp.bfloat16)
            store(b, high, low)

    def unpack_row(p, tile):
        def store(b, high, low):
            at = (tile, pl.ds((b // 2) * BLOCK, BLOCK), pl.ds((b % 2) * 128, 128))
            a_hi[at] = high
            a_lo[at] = low

        unpack(lambda u: rbuf[p, tile, u], trow, tile, store)

    def unpack_col(step, tile):
        def store(b, high, low):
            at = (
                2 * tile + b // 8,
                pl.ds((b // 2 % 4) * BLOCK, BLOCK),
                pl.ds((b % 2) * 128, 128),
            )
            b_hi[at] = high
            b_lo[at] = low

        unpack(lambda u: cbuf[step, tile, u], tcol, tile, store)

    def fold(tile):
        dot = functools.partial(jnp.dot, preferred_element_type=jnp.float32)
        total = dot(a_hi[tile], b_hi[tile])
        total = total + dot(a_lo[tile], b_hi[tile])
        total = total + dot(a_hi[tile], b_lo[tile])
        acc[...] += total


    def row_copy(p, tile, j, kind, h, dev):
        ref = rbuf.at[p, tile, pl.ds(h * HALF, HALF)]
        return pltpu.make_async_remote_copy(
            src_ref=ref,
            dst_ref=ref,
            send_sem=r_send.at[j, kind, h],
            recv_sem=r_recv.at[p, tile, h],
            device_id=dev,
            device_id_type=MESH,
        )

    def col_copy(s, tile, j, kind, h, dev):
        ref = cbuf.at[s, tile, pl.ds(h * HALF, HALF)]
        return pltpu.make_async_remote_copy(
            src_ref=ref,
            dst_ref=ref,
            send_sem=c_send.at[j, kind, h],
            recv_sem=c_recv.at[s, tile, h],
            device_id=dev,
            device_id_type=MESH,
        )


    def mid(j):
        return (j + 2) // 4 % 2

    def hop(j):
        return mid(j) * (3 - 2 * (j % 2)) + (1 - mid(j)) * 2 * (j // 6)

    def swap(j):
        return mid(j) * (j // 2 - 1) + (1 - mid(j)) * (j % 2)

    def row_tile(j):
        return 4 * ((z + hop(j)) % 4) + 2 * core + (sec + swap(j)) % 2

    def peer_tile(j):
        return 4 * ((z + hop(j)) % 4) + 2 * (1 - core) + (sec + swap(j)) % 2

    def col_tile(j):
        return 4 * ((hi + swap(j)) % 2) + (y + hop(j)) % 4

    def across_copy(p, s, h):
        piece = pl.ds(h * HALF, HALF)
        return pltpu.make_async_remote_copy(
            src_ref=rbuf.at[p, row_tile(1), piece],
            dst_ref=cbuf.at[s, row, piece],
            send_sem=c_send.at[0, 2, h],
            recv_sem=c_recv.at[s, row, h],
            device_id=across,
            device_id_type=MESH,
        )

    def row_out(p, j, h, act):
        tile = row_tile(j)

        if h == 0:

            @pl.when((j < 3) | ((j == 4) & (core == 0)))
            def _():
                act(row_copy(p, tile, j, 1, h, z_up))

            @pl.when((j < 2) | ((j == 5) & (core == 1)))
            def _():
                act(row_copy(p, tile, j, 2, h, z_down))

            @pl.when(j == 0)
            def _():
                act(row_copy(p, tile, j, 3, h, x_peer))

        else:

            @pl.when(j == 0)
            def _():
                act(row_copy(p, tile, j, 1, h, z_up))

            @pl.when((j == 0) | (j == 3))
            def _():
                act(row_copy(p, tile, j, 2, h, z_down))

            @pl.when((j == 0) | (j == 2) | (j == 3) | (j == 6))
            def _():
                act(row_copy(p, tile, j, 3, h, x_peer))

        act(row_copy(p, tile, j, 0, h, sibling))

    def col_out(s, j, h, act):
        tile = col_tile(j)
        up, down = ((j < 3) | (j == 4), j < 2) if h == 0 else (j < 2, (j < 2) | (j == 3) | (j == 5))

        @pl.when(up)
        def _():
            act(col_copy(s, tile, j, 0, h, y_up))

        @pl.when(down)
        def _():
            act(col_copy(s, tile, j, 1, h, y_down))

    def start(copy):
        copy.start()

    def drain(copy):
        copy.wait_send()

    def row_in(p, tile, h):
        row_copy(p, tile, 0, 0, h, sibling).wait_recv()

    def col_in(s, tile, h):
        col_copy(s, tile, 0, 0, h, y_up).wait_recv()

    def row_drain(p):
        def one(j, c):
            for h in range(2):
                row_out(p, j, h, drain)
            return c

        lax.fori_loop(0, 8, one, 0)

    def col_drain(p, s):
        def one(j, c):
            for h in range(2):
                col_out(s, j, h, drain)
            return c

        lax.fori_loop(0, 6, one, 0)
        for h in range(2):
            across_copy(p, s, h).wait_send()

    def small(src, dst, send, recv, dev):
        return pltpu.make_async_remote_copy(
            src_ref=src, dst_ref=dst, send_sem=send, recv_sem=recv,
            device_id=dev, device_id_type=MESH,
        )

    def loop(first, last, f):
        def one(d, c):
            f(d)
            return c

        lax.fori_loop(first, last, one, 0)


    for b in range(16):
        put(cur, b, core_ref[pl.ds((b // 2) * BLOCK, BLOCK), pl.ds((b % 2) * 128, 128)])

    def keep_iterate(p, s):
        def store(u, value):
            rbuf[p, me, u] = value
            cbuf[s, row, u] = value

        compact(cur, store)

    inv_copy.wait()
    coef_copy.wait()
    keep_iterate(0, 0)
    work[PAIRS] = jnp.zeros((BLOCK, 128), jnp.float32)
    work[2 * PAIRS + 1] = jnp.zeros((BLOCK, 128), jnp.float32)
    hrow[me] = hdr_ref[...]
    hcol[row] = hdr_ref[...]

    pl.semaphore_wait(barrier, TILES + ROWS - 1)

    def hr_copy(d):
        return small(hdr_ref, hrow.at[me], hr_send.at[d], hr_recv.at[me], row_mate(d))

    def hc_copy(d):
        return small(hdr_ref, hcol.at[row], hc_send.at[d], hc_recv.at[row], col_mate(d))

    loop(1, TILES, lambda d: hr_copy(d).start())
    loop(1, ROWS, lambda d: hc_copy(d).start())

    def read_tables():
        def wait_row(d):
            other = (me + d) % TILES
            small(hdr_ref, hrow.at[other], hr_send.at[d], hr_recv.at[other], row_mate(d)).wait_recv()

        def wait_col(d):
            other = (row + d) % ROWS
            small(hdr_ref, hcol.at[other], hc_send.at[d], hc_recv.at[other], col_mate(d)).wait_recv()

        loop(1, TILES, wait_row)
        loop(1, ROWS, wait_col)
        one = pltpu.make_async_copy(hrow, trow, t_sem.at[0])
        two = pltpu.make_async_copy(hcol, tcol, t_sem.at[1])
        one.start()
        two.start()
        one.wait()
        two.wait()


    def spread_sites():
        for a in range(4):
            for c in range(4):
                if a < 3:
                    line = sites_ref[a : a + 1, c * 128 : (c + 1) * 128]
                else:
                    line = charges_ref[0:1, c * 128 : (c + 1) * 128]
                fan[a, c * 128 : (c + 1) * 128, :] = jnp.transpose(
                    jnp.broadcast_to(line, (128, 128))
                )

    def field_chunk(ch):
        at = pl.ds(pl.multiple_of(ch * CHUNK, CHUNK), CHUNK)
        px = centers_ref[0:1, at]
        py = centers_ref[1:2, at]
        pz = centers_ref[2:3, at]

        def some(m, total):
            part = pl.ds(m * 32, 32)
            dx = fan[0, part, :] - px
            dy = fan[1, part, :] - py
            dz = fan[2, part, :] - pz
            distance = dx * dx + dy * dy + dz * dz
            value = amp_ref[0] * jnp.exp2(distance * coef_ref[0, 0])
            for g in range(1, 6):
                value = value + amp_ref[g] * jnp.exp2(distance * coef_ref[0, g])
            return total + value * fan[3, part, :]

        total = lax.fori_loop(0, 16, some, jnp.zeros((32, 128), jnp.float32), unroll=4)
        f_own[ch // 4, pl.ds(ch % 4, 1), :] = jnp.sum(total, axis=0, keepdims=True)

    def f1_copy(d):
        other = (row + d) % ROWS
        return small(f_own.at[other], f_one.at[row], f1_send.at[d], f1_recv.at[row], col_mate(d))

    def f1_wait(d):
        other = (row + d) % ROWS
        small(f_own.at[row], f_one.at[other], f1_send.at[d], f1_recv.at[other], col_mate(d)).wait_recv()

    def f2_copy(d):
        return small(f_sum, f_two.at[me], f2_send.at[d], f2_recv.at[me], row_mate(d))

    def f2_wait(d):
        other = (me + d) % TILES
        small(f_sum, f_two.at[other], f2_send.at[d], f2_recv.at[other], row_mate(d)).wait_recv()

    def f3_copy(d):
        return small(f_all, f_three.at[row], f3_send.at[d], f3_recv.at[row], col_mate(d))

    def f3_wait(d):
        other = (row + d) % ROWS
        small(f_all, f_three.at[other], f3_send.at[d], f3_recv.at[other], col_mate(d)).wait_recv()

    line8 = lax.broadcasted_iota(jnp.int32, (8, 128), 0)

    def field_first():
        f_one[row] = f_own[row]
        loop(1, ROWS, lambda d: f1_copy(d).start())

    def field_second():
        loop(1, ROWS, f1_wait)
        total = f_one[0]
        for r in range(1, ROWS):
            total = total + f_one[r]
        count = jnp.broadcast_to(hdr_ref[...], (8, 128)).astype(jnp.float32)
        total = jnp.where(line8 < 4, total, count)
        f_sum[...] = total
        f_two[me] = total
        loop(1, TILES, lambda d: f2_copy(d).start())

    def field_third():
        loop(1, TILES, f2_wait)
        total = f_two[0]
        most = f_two[0]
        for c in range(1, TILES):
            value = f_two[c]
            total = total + value
            most = jnp.maximum(most, value)
        total = jnp.where(line8 < 4, total, most)
        f_all[...] = total
        f_three[row] = total
        loop(1, ROWS, lambda d: f3_copy(d).start())

    def field_last():
        loop(1, ROWS, f3_wait)
        most = f_three[0]
        for r in range(1, ROWS):
            most = jnp.maximum(most, f_three[r])
        flag_ref[0, 0] = jnp.max(jnp.where(lane1 == 127, most[4:5, :], 0.0)).astype(jnp.int32)
        for c in range(4):
            line = f_three[row, c : c + 1, :]
            fi_col[c * 128 : (c + 1) * 128, :] = jnp.transpose(jnp.broadcast_to(line, (128, 128)))
        loop(1, ROWS, lambda d: f1_copy(d).wait_send())
        loop(1, TILES, lambda d: f2_copy(d).wait_send())
        loop(1, ROWS, lambda d: f3_copy(d).wait_send())
        loop(1, TILES, lambda d: hr_copy(d).wait_send())
        loop(1, ROWS, lambda d: hc_copy(d).wait_send())


    def one_step(step, carry):
        p = 2 * step
        first = step == 0

        def arrive(j):
            for h in range(2):

                @pl.when(j > 0)
                def _():
                    row_in(p, row_tile(j), h)

                row_out(p, j, h, start)

                @pl.when(j == 1)
                def _():
                    across_copy(p, step, h).start()

                @pl.when(j > 0)
                def _():
                    col_in(step, col_tile(j), h)

                col_out(step, j, h, start)

            @pl.when(first)
            def _():
                @pl.when(j == 0)
                def _():
                    spread_sites()
                    loop(0, 14, field_chunk)
                    read_tables()

                @pl.when((j == 1) | (j == 2))
                def _():
                    loop(9 * j + 5, 9 * j + 14, field_chunk)

                @pl.when(j == 2)
                def _():
                    field_first()

                @pl.when(j == 4)
                def _():
                    field_second()

                @pl.when(j == 6)
                def _():
                    field_third()

            unpack_row(p, row_tile(j))
            unpack_col(step, col_tile(j))

            @pl.when(j > 0)
            def _():
                peer_in(p, j - 1)

        def peer_in(q, j):
            for h in range(2):
                row_in(q, peer_tile(j), h)
            unpack_row(q, peer_tile(j))

        loop(0, 8, arrive)
        acc[...] = jnp.zeros_like(acc)
        loop(0, 8, lambda j: fold(row_tile(j)))
        loop(0, 7, lambda j: fold(peer_tile(j)))
        peer_in(p, 7)
        fold(peer_tile(7))

        @pl.when(first)
        def _():
            field_last()

        scale = jnp.where(first, 1.0, 0.0)

        def pieces(b):
            at = (pl.ds((b // 2) * BLOCK, BLOCK), pl.ds((b % 2) * 128, 128))
            fi = scale * fi_col[pl.ds((b // 2) * BLOCK, BLOCK), :]
            fj = scale * f_three[me // 2, pl.ds((me % 2) * 2 + b % 2, 1), :]
            same = (sub + (512 * row + (b // 2) * BLOCK)) == (lane + (256 * me + (b % 2) * 128))
            return at, fi, fj, same

        for b in range(16):
            at, fi, fj, same = pieces(b)
            value = acc[at] + (fi + fj) * cur[b] + jnp.where(same, fi * fi, 0.0)
            put(sq, b, value)

        def store(u, value):
            rbuf[p + 1, me, u] = value

        compact(sq, store)
        row_drain(p)

        acc[...] = jnp.zeros_like(acc)

        def arrive_square(j):
            for h in range(2):

                @pl.when(j > 0)
                def _():
                    row_in(p + 1, row_tile(j), h)

                row_out(p + 1, j, h, start)

            unpack_row(p + 1, row_tile(j))
            fold(row_tile(j))

            @pl.when(j > 0)
            def _():
                peer_in(p + 1, j - 1)
                fold(peer_tile(j - 1))

        loop(0, 8, arrive_square)
        peer_in(p + 1, 7)
        fold(peer_tile(7))

        for b in range(16):
            at, fi, fj, same = pieces(b)
            value = 1.5 * (cur[b] + jnp.where(same, fi, 0.0)) - 0.5 * (acc[at] + sq[b] * fj)
            put(cur, b, value)

        row_drain(p + 1)
        col_drain(p, step)

        @pl.when(step + 1 < STEPS)
        def _():
            keep_iterate(p + 2, step + 1)

        return carry

    lax.fori_loop(0, STEPS, one_step, 0)

    for b in range(16):
        at = (pl.ds((b // 2) * BLOCK, BLOCK), pl.ds((b % 2) * 128, 128))
        keep_left = keep_ref[b // 2, 2 * (b % 2)].astype(jnp.float32)
        keep_right = keep_ref[b // 2, 2 * (b % 2) + 1].astype(jnp.float32)
        out_ref[at] = cur[b] * jnp.where(left, keep_left, keep_right)


def body(centers, charge_sites, charges, amplitudes, widths, core_matrix, pattern):
    vmem = pl.BlockSpec(memory_space=pltpu.VMEM)
    smem = pl.BlockSpec(memory_space=pltpu.SMEM)
    f32, bf16 = jnp.float32, jnp.bfloat16
    dma = pltpu.SemaphoreType.DMA
    out, flag = pl.pallas_call(
        kernel,
        out_shape=(
            jax.ShapeDtypeStruct((512, 256), f32),
            jax.ShapeDtypeStruct((1, 1), jnp.int32),
        ),
        in_specs=[smem, smem, smem, vmem, vmem, vmem, vmem],
        out_specs=(vmem, smem),
        scratch_shapes=[
            pltpu.VMEM((4, TILES, PAIRS, BLOCK, 128), f32),
            pltpu.VMEM((2, ROWS, PAIRS, BLOCK, 128), f32),
            pltpu.VMEM((TILES, 512, 256), bf16),
            pltpu.VMEM((TILES, 512, 256), bf16),
            pltpu.VMEM((TILES, 256, 256), bf16),
            pltpu.VMEM((TILES, 256, 256), bf16),
            pltpu.VMEM((512, 256), f32),
            pltpu.VMEM((2 * PAIRS + 2, BLOCK, 128), f32),
            pltpu.VMEM((32, BLOCK, 128), f32),
            pltpu.VMEM((32, BLOCK, 128), f32),
            pltpu.VMEM((4, 512, 128), f32),
            pltpu.VMEM((ROWS, 8, 128), f32),
            pltpu.VMEM((ROWS, 8, 128), f32),
            pltpu.VMEM((TILES, 8, 128), f32),
            pltpu.VMEM((ROWS, 8, 128), f32),
            pltpu.VMEM((8, 128), f32),
            pltpu.VMEM((8, 128), f32),
            pltpu.VMEM((512, 128), f32),
            pltpu.VMEM((1, 128), jnp.int32),
            pltpu.VMEM((1, 128), jnp.int32),
            pltpu.VMEM((1, 128), f32),
            pltpu.VMEM((TILES, 1, 128), jnp.int32),
            pltpu.VMEM((ROWS, 1, 128), jnp.int32),
            pltpu.SMEM((1, 128), jnp.int32),
            pltpu.SMEM((1, 128), f32),
            pltpu.SMEM((TILES, 1, 128), jnp.int32),
            pltpu.SMEM((ROWS, 1, 128), jnp.int32),
            dma((8, 4, 2)),
            dma((4, TILES, 2)),
            dma((8, 3, 2)),
            dma((2, ROWS, 2)),
            dma((TILES,)),
            dma((TILES,)),
            dma((ROWS,)),
            dma((ROWS,)),
            dma((ROWS,)),
            dma((ROWS,)),
            dma((TILES,)),
            dma((TILES,)),
            dma((ROWS,)),
            dma((ROWS,)),
            dma((2,)),
        ],
        compiler_params=pltpu.CompilerParams(
            collective_id=0, has_side_effects=True, vmem_limit_bytes=58 * 1024 * 1024
        ),
    )(
        pattern,
        amplitudes,
        widths,
        centers,
        charge_sites,
        charges[None, :],
        core_matrix,
    )
    return lax.cond(
        flag[0, 0] > CAP,
        lambda: dense_body(
            centers, charge_sites, charges, amplitudes, widths, core_matrix, pattern
        ),
        lambda: out,
    )


def solution(mesh):
    return jax.shard_map(
        body,
        mesh=mesh,
        in_specs=(
            P(),
            P(None, AXES),
            P(AXES),
            P(),
            P(),
            P("row", ("col", "sec")),
            P("row", ("col", "sec")),
        ),
        out_specs=P("row", ("col", "sec")),
        check_vma=False,
    )
```

```python
import functools

import jax
import jax.numpy as jnp
from jax import lax
from jax.experimental import pallas as pl
from jax.experimental.pallas import tpu as pltpu
from jax.sharding import PartitionSpec as P

BLOCK = 64
STEPS = 2
ROWS, COLS, SECS = 8, 8, 2
TILES = COLS * SECS
CAP = 20
FULL = 32
CHUNK = 128
LOG2E = 1.4426950408889634
MESH = pl.DeviceIdType.MESH
AXES = ("row", "col", "sec")


def kernel(
    cap,
    keep_ref,
    amp_ref,
    width_ref,
    centers_ref,
    sites_ref,
    charges_ref,
    core_ref,
    out_ref,
    flag_ref,
    rbuf,
    cbuf,
    a_hi,
    a_lo,
    b_hi,
    b_lo,
    acc,
    work,
    cur,
    sq,
    fan,
    f_own,
    f_one,
    f_two,
    f_three,
    f_sum,
    f_all,
    fi_col,
    hdr_ref,
    inv_line,
    coef_line,
    hrow,
    hcol,
    inv_ref,
    coef_ref,
    trow,
    tcol,
    r_send,
    r_recv,
    c_send,
    c_recv,
    hr_send,
    hr_recv,
    hc_send,
    hc_recv,
    f1_send,
    f1_recv,
    f2_send,
    f2_recv,
    f3_send,
    f3_recv,
    t_sem,
):
    pairs = cap // 2
    half = pairs // 2
    row, col, sec = lax.axis_index("row"), lax.axis_index("col"), lax.axis_index("sec")
    hi, y = row // 4, row % 4
    z, core = col // 2, col % 2
    me = 2 * col + sec

    sibling = (row, 2 * z + (1 - core), sec)
    x_peer = (row, col, 1 - sec)
    z_up = (row, 2 * ((z + 1) % 4) + core, sec)
    z_down = (row, 2 * ((z + 3) % 4) + core, sec)
    across = ((row + 4) % 8, col, 1 - sec)
    y_up = (4 * hi + (y + 1) % 4, col, sec)
    y_down = (4 * hi + (y + 3) % 4, col, sec)

    def row_mate(d):
        other = (me + d) % TILES
        return (row, other // 2, other % 2)

    def col_mate(d):
        return ((row + d) % ROWS, col, sec)

    lane = lax.broadcasted_iota(jnp.int32, (BLOCK, 128), 1)
    sub = lax.broadcasted_iota(jnp.int32, (BLOCK, 128), 0)
    left = lane < BLOCK

    barrier = pltpu.get_barrier_semaphore()

    def greet_row(d, c):
        pl.semaphore_signal(barrier, inc=1, device_id=row_mate(d), device_id_type=MESH)
        return c

    def greet_col(d, c):
        pl.semaphore_signal(barrier, inc=1, device_id=col_mate(d), device_id_type=MESH)
        return c

    lax.fori_loop(1, TILES, greet_row, 0)
    lax.fori_loop(1, ROWS, greet_col, 0)
    pl.semaphore_signal(barrier, inc=1, device_id=across, device_id_type=MESH)


    lane1 = lax.broadcasted_iota(jnp.int32, (1, 128), 1)
    before = 0
    codes = jnp.full((1, 128), pairs, jnp.int32)
    blocks = jnp.zeros((1, 128), jnp.int32)
    for b in range(32):
        keep = keep_ref[b // 4, b % 4]
        turned = (before + b) % 2
        there = before // 2 + (pairs + 1) * turned
        code = jnp.where((keep == 1) & (before < cap), there, pairs)
        codes = jnp.where(lane1 == b, code, codes)
        at = jnp.where(keep == 1, before, 127)
        blocks = jnp.where(lane1 == at, b // 2 + 16 * turned, blocks)
        before = before + keep
    hdr_ref[...] = jnp.where(lane1 == 127, before, codes)
    inv_line[...] = jnp.where(lane1 < cap, blocks, 0)
    scale_line = jnp.zeros((1, 128), jnp.float32)
    for g in range(6):
        wide = jnp.full((1, 128), width_ref[g], jnp.float32)
        scale_line = jnp.where(lane1 == g, -LOG2E / (wide * wide), scale_line)
    coef_line[...] = scale_line
    inv_copy = pltpu.make_async_copy(inv_line, inv_ref, t_sem.at[0])
    coef_copy = pltpu.make_async_copy(coef_line, coef_ref, t_sem.at[1])
    inv_copy.start()
    coef_copy.start()


    def put(dst, number, value):
        dst[number] = value
        dst[16 + number] = pltpu.roll(value, BLOCK, 1)

    def compact(src, store):
        for u in range(pairs):
            value = jnp.where(left, src[inv_ref[0, 2 * u]], src[inv_ref[0, 2 * u + 1]])
            store(u, value)

    def unpack(load, table, tile, store):
        for u in range(pairs):
            value = load(u)
            work[u] = value
            work[pairs + 1 + u] = pltpu.roll(value, BLOCK, 1)
        for b in range(16):
            value = jnp.where(
                left, work[table[tile, 0, 2 * b]], work[table[tile, 0, 2 * b + 1]]
            )
            high = value.astype(jnp.bfloat16)
            low = (value - high.astype(jnp.float32)).astype(jnp.bfloat16)
            store(b, high, low)

    def unpack_row(p, tile):
        def store(b, high, low):
            at = (tile, pl.ds((b // 2) * BLOCK, BLOCK), pl.ds((b % 2) * 128, 128))
            a_hi[at] = high
            a_lo[at] = low

        unpack(lambda u: rbuf[p % 2, tile, u], trow, tile, store)

    def unpack_col(step, tile):
        def store(b, high, low):
            at = (
                2 * tile + b // 8,
                pl.ds((b // 2 % 4) * BLOCK, BLOCK),
                pl.ds((b % 2) * 128, 128),
            )
            b_hi[at] = high
            b_lo[at] = low

        unpack(lambda u: cbuf[step, tile, u], tcol, tile, store)

    def fold(tile):
        dot = functools.partial(jnp.dot, preferred_element_type=jnp.float32)
        total = dot(a_hi[tile], b_hi[tile])
        total = total + dot(a_lo[tile], b_hi[tile])
        total = total + dot(a_hi[tile], b_lo[tile])
        acc[...] += total


    def row_copy(p, tile, j, kind, h, dev):
        ref = rbuf.at[p % 2, tile, pl.ds(h * half, half)]
        return pltpu.make_async_remote_copy(
            src_ref=ref,
            dst_ref=ref,
            send_sem=r_send.at[j, kind, h],
            recv_sem=r_recv.at[p, tile, h],
            device_id=dev,
            device_id_type=MESH,
        )

    def col_copy(s, tile, j, kind, h, dev):
        ref = cbuf.at[s, tile, pl.ds(h * half, half)]
        return pltpu.make_async_remote_copy(
            src_ref=ref,
            dst_ref=ref,
            send_sem=c_send.at[j, kind, h],
            recv_sem=c_recv.at[s, tile, h],
            device_id=dev,
            device_id_type=MESH,
        )


    def mid(j):
        return (j + 2) // 4 % 2

    def hop(j):
        return mid(j) * (3 - 2 * (j % 2)) + (1 - mid(j)) * 2 * (j // 6)

    def swap(j):
        return mid(j) * (j // 2 - 1) + (1 - mid(j)) * (j % 2)

    def row_tile(j):
        return 4 * ((z + hop(j)) % 4) + 2 * core + (sec + swap(j)) % 2

    def peer_tile(j):
        return 4 * ((z + hop(j)) % 4) + 2 * (1 - core) + (sec + swap(j)) % 2

    def col_tile(j):
        return 4 * ((hi + swap(j)) % 2) + (y + hop(j)) % 4

    def across_copy(p, s, h):
        piece = pl.ds(h * half, half)
        return pltpu.make_async_remote_copy(
            src_ref=rbuf.at[p % 2, row_tile(1), piece],
            dst_ref=cbuf.at[s, row, piece],
            send_sem=c_send.at[0, 2, h],
            recv_sem=c_recv.at[s, row, h],
            device_id=across,
            device_id_type=MESH,
        )

    row_plan = {
        (0, 0): (1, 2, 3, 0),
        (0, 1): (1, 2, 3, 0),
        (1, 0): (0,),
        (1, 1): (1, 2, 0),
        (2, 0): (1, 3, 0),
        (2, 1): (0,),
        (3, 0): (3, 0),
        (3, 1): (2, 0),
        (4, 0): (0,),
        (4, 1): (1, 0),
        (5, 0): (0,),
        (5, 1): (2, 0),
        (6, 0): (3, 0),
        (6, 1): (0,),
        (7, 0): (0,),
        (7, 1): (0,),
    }
    col_plan = {
        (0, 0): (0, 1),
        (0, 1): (0, 1),
        (1, 0): (0, 1),
        (1, 1): (0, 1),
        (2, 0): (0,),
        (3, 1): (1,),
        (4, 0): (0,),
        (5, 1): (1,),
    }
    row_to = (sibling, z_up, z_down, x_peer)
    col_to = (y_up, y_down)

    def row_act(p, j, h, kind, act):
        def go():
            act(row_copy(p, row_tile(j), j, kind, h, row_to[kind]))

        if j in (4, 5) and kind > 0:
            pl.when(core == j - 4)(go)
        else:
            go()

    def col_act(s, j, h, kind, act):
        act(col_copy(s, col_tile(j), j, kind, h, col_to[kind]))

    def start(copy):
        copy.start()

    def row_pass(p, *pieces):
        for j, h in pieces:
            if j > 0:
                row_in(p, row_tile(j), h)
            for kind in row_plan[j, h]:
                row_act(p, j, h, kind, start)

    def col_pass(s, *pieces):
        for j, h in pieces:
            if j > 0:
                col_in(s, col_tile(j), h)
            for kind in col_plan[j, h]:
                col_act(s, j, h, kind, start)

    def drain(copy):
        copy.wait_send()

    def row_in(p, tile, h):
        row_copy(p, tile, 0, 0, h, sibling).wait_recv()

    def col_in(s, tile, h):
        col_copy(s, tile, 0, 0, h, y_up).wait_recv()

    def row_drain(p):
        for (j, h), kinds in row_plan.items():
            for kind in kinds:
                row_act(p, j, h, kind, drain)

    def col_drain(s):
        for (j, h), kinds in col_plan.items():
            for kind in kinds:
                col_act(s, j, h, kind, drain)

    def small(src, dst, send, recv, dev):
        return pltpu.make_async_remote_copy(
            src_ref=src, dst_ref=dst, send_sem=send, recv_sem=recv,
            device_id=dev, device_id_type=MESH,
        )

    def loop(first, last, f):
        def one(d, c):
            f(d)
            return c

        lax.fori_loop(first, last, one, 0)


    for b in range(16):
        put(cur, b, core_ref[pl.ds((b // 2) * BLOCK, BLOCK), pl.ds((b % 2) * 128, 128)])

    def keep_iterate(p, s):
        def store(u, value):
            rbuf[p % 2, me, u] = value
            cbuf[s, row, u] = value

        compact(cur, store)

    inv_copy.wait()
    coef_copy.wait()
    keep_iterate(0, 0)
    work[pairs] = jnp.zeros((BLOCK, 128), jnp.float32)
    work[2 * pairs + 1] = jnp.zeros((BLOCK, 128), jnp.float32)
    hrow[me] = hdr_ref[...]
    hcol[row] = hdr_ref[...]

    pl.semaphore_wait(barrier, TILES + ROWS - 1)

    def hr_copy(d):
        return small(hdr_ref, hrow.at[me], hr_send.at[d], hr_recv.at[me], row_mate(d))

    def hc_copy(d):
        return small(hdr_ref, hcol.at[row], hc_send.at[d], hc_recv.at[row], col_mate(d))

    loop(1, TILES, lambda d: hr_copy(d).start())
    loop(1, ROWS, lambda d: hc_copy(d).start())

    def read_tables():
        def wait_row(d):
            other = (me + d) % TILES
            small(hdr_ref, hrow.at[other], hr_send.at[d], hr_recv.at[other], row_mate(d)).wait_recv()

        def wait_col(d):
            other = (row + d) % ROWS
            small(hdr_ref, hcol.at[other], hc_send.at[d], hc_recv.at[other], col_mate(d)).wait_recv()

        loop(1, TILES, wait_row)
        loop(1, ROWS, wait_col)
        one = pltpu.make_async_copy(hrow, trow, t_sem.at[0])
        two = pltpu.make_async_copy(hcol, tcol, t_sem.at[1])
        one.start()
        two.start()
        one.wait()
        two.wait()


    def spread_sites():
        for a in range(4):
            for c in range(4):
                if a < 3:
                    line = sites_ref[a : a + 1, c * 128 : (c + 1) * 128]
                else:
                    line = charges_ref[0:1, c * 128 : (c + 1) * 128]
                fan[a, c * 128 : (c + 1) * 128, :] = jnp.transpose(
                    jnp.broadcast_to(line, (128, 128))
                )

    def field_chunk(ch):
        at = pl.ds(pl.multiple_of(ch * CHUNK, CHUNK), CHUNK)
        px = centers_ref[0:1, at]
        py = centers_ref[1:2, at]
        pz = centers_ref[2:3, at]

        def some(m, total):
            part = pl.ds(m * 32, 32)
            dx = fan[0, part, :] - px
            dy = fan[1, part, :] - py
            dz = fan[2, part, :] - pz
            distance = dx * dx + dy * dy + dz * dz
            value = amp_ref[0] * jnp.exp2(distance * coef_ref[0, 0])
            for g in range(1, 6):
                value = value + amp_ref[g] * jnp.exp2(distance * coef_ref[0, g])
            return total + value * fan[3, part, :]

        total = lax.fori_loop(0, 16, some, jnp.zeros((32, 128), jnp.float32), unroll=4)
        f_own[ch // 4, pl.ds(ch % 4, 1), :] = jnp.sum(total, axis=0, keepdims=True)

    def f1_copy(d):
        other = (row + d) % ROWS
        return small(f_own.at[other], f_one.at[row], f1_send.at[d], f1_recv.at[row], col_mate(d))

    def f1_wait(d):
        other = (row + d) % ROWS
        small(f_own.at[row], f_one.at[other], f1_send.at[d], f1_recv.at[other], col_mate(d)).wait_recv()

    def f2_copy(d):
        return small(f_sum, f_two.at[me], f2_send.at[d], f2_recv.at[me], row_mate(d))

    def f2_wait(d):
        other = (me + d) % TILES
        small(f_sum, f_two.at[other], f2_send.at[d], f2_recv.at[other], row_mate(d)).wait_recv()

    def f3_copy(d):
        return small(f_all, f_three.at[row], f3_send.at[d], f3_recv.at[row], col_mate(d))

    def f3_wait(d):
        other = (row + d) % ROWS
        small(f_all, f_three.at[other], f3_send.at[d], f3_recv.at[other], col_mate(d)).wait_recv()

    line8 = lax.broadcasted_iota(jnp.int32, (8, 128), 0)

    def field_first():
        f_one[row] = f_own[row]
        loop(1, ROWS, lambda d: f1_copy(d).start())

    def field_second():
        loop(1, ROWS, f1_wait)
        total = f_one[0]
        for r in range(1, ROWS):
            total = total + f_one[r]
        count = jnp.broadcast_to(hdr_ref[...], (8, 128)).astype(jnp.float32)
        total = jnp.where(line8 < 4, total, count)
        f_sum[...] = total
        f_two[me] = total
        loop(1, TILES, lambda d: f2_copy(d).start())

    def field_third():
        loop(1, TILES, f2_wait)
        total = f_two[0]
        most = f_two[0]
        for c in range(1, TILES):
            value = f_two[c]
            total = total + value
            most = jnp.maximum(most, value)
        total = jnp.where(line8 < 4, total, most)
        f_all[...] = total
        f_three[row] = total
        loop(1, ROWS, lambda d: f3_copy(d).start())

    def field_last():
        loop(1, ROWS, f3_wait)
        most = f_three[0]
        for r in range(1, ROWS):
            most = jnp.maximum(most, f_three[r])
        flag_ref[0, 0] = jnp.max(jnp.where(lane1 == 127, most[4:5, :], 0.0)).astype(jnp.int32)
        for c in range(4):
            line = f_three[row, c : c + 1, :]
            fi_col[c * 128 : (c + 1) * 128, :] = jnp.transpose(jnp.broadcast_to(line, (128, 128)))
        loop(1, ROWS, lambda d: f1_copy(d).wait_send())
        loop(1, TILES, lambda d: f2_copy(d).wait_send())
        loop(1, ROWS, lambda d: f3_copy(d).wait_send())
        loop(1, TILES, lambda d: hr_copy(d).wait_send())
        loop(1, ROWS, lambda d: hc_copy(d).wait_send())


    def one_step(step, carry):
        p = 2 * step
        first = step == 0

        def rows_open(q, from_, to_):
            loop(from_, to_, lambda j: unpack_row(q, row_tile(j)))

        def peers_open(q, from_, to_):
            def one(j):
                for h in range(2):
                    row_in(q, peer_tile(j), h)
                unpack_row(q, peer_tile(j))

            loop(from_, to_, one)

        def once(*acts):
            @pl.when(first)
            def _():
                for act in acts:
                    act()

        def chunks(from_, to_):
            return lambda: loop(from_, to_, field_chunk)

        for h in range(2):
            row_pass(p, (0, h))
            col_pass(step, (0, h))
        once(spread_sites, chunks(0, 9), read_tables)
        rows_open(p, 0, 1)
        unpack_col(step, col_tile(0))
        col_pass(step, (2, 0))
        row_pass(p, (2, 0), (3, 0), (1, 0))
        across_copy(p, step, 0).start()
        once(chunks(9, 18))
        row_pass(p, (3, 1), (1, 1))
        across_copy(p, step, 1).start()
        col_pass(step, (3, 1))
        row_pass(p, (2, 1))
        once(chunks(18, 26))
        rows_open(p, 1, 4)
        col_pass(step, (1, 0))
        row_pass(p, (6, 0))
        col_pass(step, (1, 1))
        once(chunks(26, 32), field_first)
        unpack_col(step, col_tile(1))
        row_pass(p, (4, 0), (6, 1), (4, 1))
        peers_open(p, 0, 3)
        row_pass(p, (5, 1), (5, 0))
        col_in(step, col_tile(2), 1)
        col_in(step, col_tile(3), 0)
        loop(2, 4, lambda j: unpack_col(step, col_tile(j)))
        col_pass(step, (4, 0), (5, 1))
        once(field_second)
        rows_open(p, 4, 7)
        row_pass(p, (7, 0), (7, 1))
        peers_open(p, 3, 6)
        rows_open(p, 7, 8)
        col_in(step, col_tile(4), 1)
        col_in(step, col_tile(5), 0)
        for h in range(2):
            col_in(step, col_tile(6), h)
        loop(4, 7, lambda j: unpack_col(step, col_tile(j)))
        once(field_third)
        peers_open(p, 6, 7)
        acc[...] = jnp.zeros_like(acc)
        last_row, last_col = peer_tile(7), col_tile(7)

        def early(t):
            @pl.when((t // 2 != last_col) & (t != last_row))
            def _():
                fold(t)

        loop(0, TILES, early)
        peers_open(p, 7, 8)

        @pl.when(last_row // 2 != last_col)
        def _():
            fold(last_row)

        for h in range(2):
            col_in(step, col_tile(7), h)
        unpack_col(step, col_tile(7))
        loop(0, 2, lambda i: fold(2 * last_col + i))
        once(field_last)

        scale = jnp.where(first, 1.0, 0.0)

        def pieces(b):
            at = (pl.ds((b // 2) * BLOCK, BLOCK), pl.ds((b % 2) * 128, 128))
            fi = scale * fi_col[pl.ds((b // 2) * BLOCK, BLOCK), :]
            fj = scale * f_three[me // 2, pl.ds((me % 2) * 2 + b % 2, 1), :]
            same = (sub + (512 * row + (b // 2) * BLOCK)) == (lane + (256 * me + (b % 2) * 128))
            return at, fi, fj, same

        for b in range(16):
            at, fi, fj, same = pieces(b)
            value = acc[at] + (fi + fj) * cur[b] + jnp.where(same, fi * fi, 0.0)
            put(sq, b, value)

        def store(u, value):
            rbuf[1, me, u] = value

        compact(sq, store)
        row_drain(p)
        for h in range(2):
            across_copy(p, step, h).wait_send()

        acc[...] = jnp.zeros_like(acc)

        def rows_fold(from_, to_):
            def one(j):
                unpack_row(p + 1, row_tile(j))
                fold(row_tile(j))

            loop(from_, to_, one)

        def peers_fold(from_, to_):
            def one(j):
                for h in range(2):
                    row_in(p + 1, peer_tile(j), h)
                unpack_row(p + 1, peer_tile(j))
                fold(peer_tile(j))

            loop(from_, to_, one)

        row_pass(p + 1, (0, 0), (0, 1))
        rows_fold(0, 1)
        row_pass(p + 1, (2, 0), (3, 0), (1, 0))
        row_pass(p + 1, (3, 1), (1, 1), (2, 1))
        peers_fold(0, 1)
        rows_fold(1, 4)
        row_pass(p + 1, (6, 0), (4, 0), (6, 1))
        peers_fold(1, 4)
        row_pass(p + 1, (4, 1), (5, 1), (5, 0))
        rows_fold(4, 7)
        row_pass(p + 1, (7, 1), (7, 0))
        peers_fold(4, 7)
        rows_fold(7, 8)
        peers_fold(7, 8)

        for b in range(16):
            at, fi, fj, same = pieces(b)
            value = 1.5 * (cur[b] + jnp.where(same, fi, 0.0)) - 0.5 * (acc[at] + sq[b] * fj)
            put(cur, b, value)

        row_drain(p + 1)
        col_drain(step)

        @pl.when(step + 1 < STEPS)
        def _():
            keep_iterate(p + 2, step + 1)

        return carry

    lax.fori_loop(0, STEPS, one_step, 0)

    for b in range(16):
        at = (pl.ds((b // 2) * BLOCK, BLOCK), pl.ds((b % 2) * 128, 128))
        keep_left = keep_ref[b // 2, 2 * (b % 2)].astype(jnp.float32)
        keep_right = keep_ref[b // 2, 2 * (b % 2) + 1].astype(jnp.float32)
        out_ref[at] = cur[b] * jnp.where(left, keep_left, keep_right)


def run(cap, number, *operands):
    pairs = cap // 2
    vmem = pl.BlockSpec(memory_space=pltpu.VMEM)
    smem = pl.BlockSpec(memory_space=pltpu.SMEM)
    f32, bf16 = jnp.float32, jnp.bfloat16
    dma = pltpu.SemaphoreType.DMA
    return pl.pallas_call(
        functools.partial(kernel, cap),
        out_shape=(
            jax.ShapeDtypeStruct((512, 256), f32),
            jax.ShapeDtypeStruct((1, 1), jnp.int32),
        ),
        in_specs=[smem, smem, smem, vmem, vmem, vmem, vmem],
        out_specs=(vmem, smem),
        scratch_shapes=[
            pltpu.VMEM((2, TILES, pairs, BLOCK, 128), f32),
            pltpu.VMEM((2, ROWS, pairs, BLOCK, 128), f32),
            pltpu.VMEM((TILES, 512, 256), bf16),
            pltpu.VMEM((TILES, 512, 256), bf16),
            pltpu.VMEM((TILES, 256, 256), bf16),
            pltpu.VMEM((TILES, 256, 256), bf16),
            pltpu.VMEM((512, 256), f32),
            pltpu.VMEM((2 * pairs + 2, BLOCK, 128), f32),
            pltpu.VMEM((32, BLOCK, 128), f32),
            pltpu.VMEM((32, BLOCK, 128), f32),
            pltpu.VMEM((4, 512, 128), f32),
            pltpu.VMEM((ROWS, 8, 128), f32),
            pltpu.VMEM((ROWS, 8, 128), f32),
            pltpu.VMEM((TILES, 8, 128), f32),
            pltpu.VMEM((ROWS, 8, 128), f32),
            pltpu.VMEM((8, 128), f32),
            pltpu.VMEM((8, 128), f32),
            pltpu.VMEM((512, 128), f32),
            pltpu.VMEM((1, 128), jnp.int32),
            pltpu.VMEM((1, 128), jnp.int32),
            pltpu.VMEM((1, 128), f32),
            pltpu.VMEM((TILES, 1, 128), jnp.int32),
            pltpu.VMEM((ROWS, 1, 128), jnp.int32),
            pltpu.SMEM((1, 128), jnp.int32),
            pltpu.SMEM((1, 128), f32),
            pltpu.SMEM((TILES, 1, 128), jnp.int32),
            pltpu.SMEM((ROWS, 1, 128), jnp.int32),
            dma((8, 4, 2)),
            dma((4, TILES, 2)),
            dma((8, 3, 2)),
            dma((2, ROWS, 2)),
            dma((TILES,)),
            dma((TILES,)),
            dma((ROWS,)),
            dma((ROWS,)),
            dma((ROWS,)),
            dma((ROWS,)),
            dma((TILES,)),
            dma((TILES,)),
            dma((ROWS,)),
            dma((ROWS,)),
            dma((2,)),
        ],
        compiler_params=pltpu.CompilerParams(
            collective_id=number, has_side_effects=True, vmem_limit_bytes=58 * 1024 * 1024
        ),
    )(*operands)


def body(centers, charge_sites, charges, amplitudes, widths, core_matrix, pattern):
    operands = (
        pattern,
        amplitudes,
        widths,
        centers,
        charge_sites,
        charges[None, :],
        core_matrix,
    )
    out, flag = run(CAP, 0, *operands)
    return lax.cond(flag[0, 0] > CAP, lambda: run(FULL, 1, *operands)[0], lambda: out)


def solution(mesh):
    return jax.shard_map(
        body,
        mesh=mesh,
        in_specs=(
            P(),
            P(None, AXES),
            P(AXES),
            P(),
            P(),
            P("row", ("col", "sec")),
            P("row", ("col", "sec")),
        ),
        out_specs=P("row", ("col", "sec")),
        check_vma=False,
    )
```

```python
import functools

import jax
import jax.numpy as jnp
from jax import lax
from jax.experimental import pallas as pl
from jax.experimental.pallas import tpu as pltpu
from jax.sharding import PartitionSpec as P

BLOCK = 64
STEPS = 2
ROWS, COLS, SECS = 8, 8, 2
TILES = COLS * SECS
CAP = 16
FULL = 32
CHUNK = 128
LOG2E = 1.4426950408889634
MESH = pl.DeviceIdType.MESH
AXES = ("row", "col", "sec")


def kernel(
    cap,
    keep_ref,
    amp_ref,
    width_ref,
    centers_ref,
    sites_ref,
    charges_ref,
    core_ref,
    out_ref,
    flag_ref,
    rbuf,
    cbuf,
    xbuf,
    over_out,
    over_in,
    a_hi,
    a_lo,
    b_hi,
    b_lo,
    acc,
    work,
    cur,
    sq,
    fan,
    f_own,
    f_one,
    f_two,
    f_three,
    f_sum,
    f_all,
    fi_col,
    hdr_ref,
    inv_line,
    coef_line,
    hrow,
    hcol,
    inv_ref,
    coef_ref,
    trow,
    tcol,
    r_send,
    r_recv,
    c_send,
    c_recv,
    x_send,
    x_recv,
    o_send,
    o_recv,
    hr_send,
    hr_recv,
    hc_send,
    hc_recv,
    f1_send,
    f1_recv,
    f2_send,
    f2_recv,
    f3_send,
    f3_recv,
    t_sem,
):
    pairs = cap // 2
    half = pairs // 2
    row, col, sec = lax.axis_index("row"), lax.axis_index("col"), lax.axis_index("sec")
    hi, y = row // 4, row % 4
    z, core = col // 2, col % 2
    me = 2 * col + sec

    sibling = (row, 2 * z + (1 - core), sec)
    x_peer = (row, col, 1 - sec)
    z_up = (row, 2 * ((z + 1) % 4) + core, sec)
    z_down = (row, 2 * ((z + 3) % 4) + core, sec)
    across = ((row + 4) % 8, col, 1 - sec)
    y_up = (4 * hi + (y + 1) % 4, col, sec)
    y_down = (4 * hi + (y + 3) % 4, col, sec)

    def row_mate(d):
        other = (me + d) % TILES
        return (row, other // 2, other % 2)

    def col_mate(d):
        return ((row + d) % ROWS, col, sec)

    lane = lax.broadcasted_iota(jnp.int32, (BLOCK, 128), 1)
    sub = lax.broadcasted_iota(jnp.int32, (BLOCK, 128), 0)
    left = lane < BLOCK

    barrier = pltpu.get_barrier_semaphore()

    def greet_row(d, c):
        pl.semaphore_signal(barrier, inc=1, device_id=row_mate(d), device_id_type=MESH)
        return c

    def greet_col(d, c):
        pl.semaphore_signal(barrier, inc=1, device_id=col_mate(d), device_id_type=MESH)
        return c

    lax.fori_loop(1, TILES, greet_row, 0)
    lax.fori_loop(1, ROWS, greet_col, 0)
    pl.semaphore_signal(barrier, inc=1, device_id=across, device_id_type=MESH)


    lane1 = lax.broadcasted_iota(jnp.int32, (1, 128), 1)
    before = 0
    empty = 2 * pairs
    codes = jnp.full((1, 128), empty, jnp.int32)
    blocks = jnp.zeros((1, 128), jnp.int32)
    for b in range(32):
        keep = keep_ref[b // 4, b % 4]
        turned = (before + b) % 2
        spare = 2 * cap - 1 - before
        own = core * pairs + before // 2 + (2 * pairs + 1) * turned
        other = (1 - core) * pairs + spare // 2 + (2 * pairs + 1) * (1 - turned)
        code = jnp.where(before < cap, own, jnp.where(spare >= cap // 2, other, empty))
        code = jnp.where(keep == 1, code, empty)
        codes = jnp.where(lane1 == b, code, codes)
        at = jnp.where(before < cap, before, jnp.where(spare >= cap // 2, 64 + spare, 127))
        at = jnp.where(keep == 1, at, 127)
        blocks = jnp.where(lane1 == at, b // 2 + 16 * ((at + b) % 2), blocks)
        before = before + keep
    hdr_ref[...] = jnp.where(lane1 == 127, before, codes)
    inv_line[...] = jnp.where(lane1 < 127, blocks, 0)
    scale_line = jnp.zeros((1, 128), jnp.float32)
    for g in range(6):
        wide = jnp.full((1, 128), width_ref[g], jnp.float32)
        scale_line = jnp.where(lane1 == g, -LOG2E / (wide * wide), scale_line)
    coef_line[...] = scale_line
    inv_copy = pltpu.make_async_copy(inv_line, inv_ref, t_sem.at[0])
    coef_copy = pltpu.make_async_copy(coef_line, coef_ref, t_sem.at[1])
    inv_copy.start()
    coef_copy.start()


    def put(dst, number, value):
        dst[number] = value
        dst[16 + number] = pltpu.roll(value, BLOCK, 1)

    def pair(src, first_slot):
        return jnp.where(left, src[inv_ref[0, first_slot]], src[inv_ref[0, first_slot + 1]])

    def over_copy(q):
        return pltpu.make_async_remote_copy(
            src_ref=over_out.at[q],
            dst_ref=over_in.at[q],
            send_sem=o_send.at[q],
            recv_sem=o_recv.at[q],
            device_id=sibling,
            device_id_type=MESH,
        )

    def spill(src, q):
        for u in range(half):
            over_out[q, u] = pair(src, 64 + 2 * (half + u))

    def compact_first(src, store):
        for u in range(half):
            store(u, pair(src, 2 * u))

    def compact_second(src, q, store):
        over_copy(q).wait()
        for u in range(half, pairs):
            slot = 2 * u + jnp.where(left, 0, 1)
            store(u, jnp.where(slot < before, pair(src, 2 * u), over_in[q, u - half]))

    def lay(number, value):
        work[number] = value
        work[2 * pairs + 1 + number] = pltpu.roll(value, BLOCK, 1)

    def unpack(table, tile, store):
        for b in range(16):
            value = jnp.where(
                left, work[table[tile, 0, 2 * b]], work[table[tile, 0, 2 * b + 1]]
            )
            high = value.astype(jnp.bfloat16)
            low = (value - high.astype(jnp.float32)).astype(jnp.bfloat16)
            store(b, high, low)

    def unpack_chip(q, tile):
        for u in range(pairs):
            lay(u, rbuf[q, tile, u])
            lay(pairs + u, rbuf[q, tile + 2, u])

        def one(i, c):
            at_tile = tile + 2 * i

            def store(b, high, low):
                at = (at_tile, pl.ds((b // 2) * BLOCK, BLOCK), pl.ds((b % 2) * 128, 128))
                a_hi[at] = high
                a_lo[at] = low

            unpack(trow, at_tile, store)
            return c

        lax.fori_loop(0, 2, one, 0)

    def unpack_col(s, tile):
        for u in range(pairs):
            lay(core * pairs + u, cbuf[s, tile, u])
        for u in range(half):
            lay((1 - core) * pairs + half + u, xbuf[s, tile, u])

        def store(b, high, low):
            at = (
                2 * tile + b // 8,
                pl.ds((b // 2 % 4) * BLOCK, BLOCK),
                pl.ds((b % 2) * 128, 128),
            )
            b_hi[at] = high
            b_lo[at] = low

        unpack(tcol, tile, store)

    def fold(*tiles):
        dot = functools.partial(jnp.dot, preferred_element_type=jnp.float32)
        total = acc[...]
        for tile in tiles:
            total = total + dot(a_hi[tile], b_hi[tile])
            total = total + dot(a_lo[tile], b_hi[tile])
            total = total + dot(a_hi[tile], b_lo[tile])
        acc[...] = total


    def row_copy(p, tile, j, kind, h, dev):
        ref = rbuf.at[p % 2, tile, pl.ds(h * half, half)]
        return pltpu.make_async_remote_copy(
            src_ref=ref,
            dst_ref=ref,
            send_sem=r_send.at[j, kind, h],
            recv_sem=r_recv.at[p, tile, h],
            device_id=dev,
            device_id_type=MESH,
        )

    def col_copy(s, tile, j, kind, h, dev):
        ref = cbuf.at[s, tile, pl.ds(h * half, half)]
        return pltpu.make_async_remote_copy(
            src_ref=ref,
            dst_ref=ref,
            send_sem=c_send.at[j, kind, h],
            recv_sem=c_recv.at[s, tile, h],
            device_id=dev,
            device_id_type=MESH,
        )


    def mid(j):
        return (j + 2) // 4 % 2

    def hop(j):
        return mid(j) * (3 - 2 * (j % 2)) + (1 - mid(j)) * 2 * (j // 6)

    def swap(j):
        return mid(j) * (j // 2 - 1) + (1 - mid(j)) * (j % 2)

    def chip_tile(j):
        return 4 * ((z + hop(j)) % 4) + (sec + swap(j)) % 2

    def row_tile(j):
        return chip_tile(j) + 2 * core

    def peer_tile(j):
        return chip_tile(j) + 2 * (1 - core)

    def col_tile(j):
        return 4 * ((hi + swap(j)) % 2) + (y + hop(j)) % 4

    def across_copy(p, s, h):
        piece = pl.ds(h * half, half)
        return pltpu.make_async_remote_copy(
            src_ref=rbuf.at[p % 2, row_tile(1), piece],
            dst_ref=cbuf.at[s, row, piece],
            send_sem=c_send.at[0, 2, h],
            recv_sem=c_recv.at[s, row, h],
            device_id=across,
            device_id_type=MESH,
        )

    def x_copy(s, j):
        tile = col_tile(j)
        return pltpu.make_async_remote_copy(
            src_ref=cbuf.at[s, tile, pl.ds(half, half)],
            dst_ref=xbuf.at[s, tile],
            send_sem=x_send.at[j],
            recv_sem=x_recv.at[s, tile],
            device_id=sibling,
            device_id_type=MESH,
        )

    row_plan = {
        (0, 0): (1, 2, 3, 0),
        (0, 1): (1, 2, 3, 0),
        (1, 0): (0,),
        (1, 1): (1, 2, 0),
        (2, 0): (1, 3, 0),
        (2, 1): (0,),
        (3, 0): (3, 0),
        (3, 1): (2, 0),
        (4, 0): (0,),
        (4, 1): (1, 0),
        (5, 0): (0,),
        (5, 1): (2, 0),
        (6, 0): (3, 0),
        (6, 1): (0,),
        (7, 0): (0,),
        (7, 1): (0,),
    }
    col_plan = {
        (0, 0): (0, 1),
        (0, 1): (0, 1),
        (1, 0): (0, 1),
        (1, 1): (0, 1),
        (2, 0): (0,),
        (2, 1): (),
        (3, 0): (),
        (3, 1): (1,),
        (4, 0): (0,),
        (4, 1): (),
        (5, 0): (),
        (5, 1): (1,),
        (6, 0): (),
        (6, 1): (),
        (7, 0): (),
        (7, 1): (),
    }
    row_to = (sibling, z_up, z_down, x_peer)
    col_to = (y_up, y_down)

    def row_act(p, j, h, kind, act):
        def go():
            act(row_copy(p, row_tile(j), j, kind, h, row_to[kind]))

        if j in (4, 5) and kind > 0:
            pl.when(core == j - 4)(go)
        else:
            go()

    def col_act(s, j, h, kind, act):
        act(col_copy(s, col_tile(j), j, kind, h, col_to[kind]))

    def start(copy):
        copy.start()

    def row_pass(p, *pieces):
        for j, h in pieces:
            if j > 0:
                row_in(p, row_tile(j), h)
            for kind in row_plan[j, h]:
                row_act(p, j, h, kind, start)

    def col_pass(s, *pieces):
        for j, h in pieces:
            if j > 0:
                col_in(s, col_tile(j), h)
            for kind in col_plan[j, h]:
                col_act(s, j, h, kind, start)
            if h == 1:
                x_copy(s, j).start()

    def drain(copy):
        copy.wait_send()

    def row_in(p, tile, h):
        row_copy(p, tile, 0, 0, h, sibling).wait_recv()

    def col_in(s, tile, h):
        col_copy(s, tile, 0, 0, h, y_up).wait_recv()

    def row_drain(p):
        for (j, h), kinds in row_plan.items():
            for kind in kinds:
                row_act(p, j, h, kind, drain)

    def col_drain(s):
        for (j, h), kinds in col_plan.items():
            for kind in kinds:
                col_act(s, j, h, kind, drain)
            if h == 1:
                x_copy(s, j).wait_send()

    def small(src, dst, send, recv, dev):
        return pltpu.make_async_remote_copy(
            src_ref=src, dst_ref=dst, send_sem=send, recv_sem=recv,
            device_id=dev, device_id_type=MESH,
        )

    def loop(first, last, f):
        def one(d, c):
            f(d)
            return c

        lax.fori_loop(first, last, one, 0)


    for b in range(16):
        put(cur, b, core_ref[pl.ds((b // 2) * BLOCK, BLOCK), pl.ds((b % 2) * 128, 128)])

    def keep_iterate(s):
        def store(u, value):
            rbuf[0, me, u] = value
            cbuf[s, row, u] = value

        return store

    inv_copy.wait()
    coef_copy.wait()
    spill(cur, 0)
    compact_first(cur, keep_iterate(0))
    work[empty] = jnp.zeros((BLOCK, 128), jnp.float32)
    work[4 * pairs + 1] = jnp.zeros((BLOCK, 128), jnp.float32)
    hrow[me] = hdr_ref[...]
    hcol[row] = hdr_ref[...]

    def hr_copy(d):
        return small(hdr_ref, hrow.at[me], hr_send.at[d], hr_recv.at[me], row_mate(d))

    def hc_copy(d):
        return small(hdr_ref, hcol.at[row], hc_send.at[d], hc_recv.at[row], col_mate(d))

    pl.semaphore_wait(barrier, TILES + ROWS - 1)
    loop(1, TILES, lambda d: hr_copy(d).start())
    loop(1, ROWS, lambda d: hc_copy(d).start())

    def read_tables():
        def wait_row(d):
            other = (me + d) % TILES
            small(hdr_ref, hrow.at[other], hr_send.at[d], hr_recv.at[other], row_mate(d)).wait_recv()

        def wait_col(d):
            other = (row + d) % ROWS
            small(hdr_ref, hcol.at[other], hc_send.at[d], hc_recv.at[other], col_mate(d)).wait_recv()

        loop(1, TILES, wait_row)
        loop(1, ROWS, wait_col)
        one = pltpu.make_async_copy(hrow, trow, t_sem.at[0])
        two = pltpu.make_async_copy(hcol, tcol, t_sem.at[1])
        one.start()
        two.start()
        one.wait()
        two.wait()


    def spread_sites():
        for a in range(4):
            for c in range(4):
                if a < 3:
                    line = sites_ref[a : a + 1, c * 128 : (c + 1) * 128]
                else:
                    line = charges_ref[0:1, c * 128 : (c + 1) * 128]
                fan[a, c * 128 : (c + 1) * 128, :] = jnp.transpose(
                    jnp.broadcast_to(line, (128, 128))
                )

    def field_chunk(ch):
        at = pl.ds(pl.multiple_of(ch * CHUNK, CHUNK), CHUNK)
        px = centers_ref[0:1, at]
        py = centers_ref[1:2, at]
        pz = centers_ref[2:3, at]

        def some(m, total):
            part = pl.ds(m * 32, 32)
            dx = fan[0, part, :] - px
            dy = fan[1, part, :] - py
            dz = fan[2, part, :] - pz
            distance = dx * dx + dy * dy + dz * dz
            value = amp_ref[0] * jnp.exp2(distance * coef_ref[0, 0])
            for g in range(1, 6):
                value = value + amp_ref[g] * jnp.exp2(distance * coef_ref[0, g])
            return total + value * fan[3, part, :]

        total = lax.fori_loop(0, 16, some, jnp.zeros((32, 128), jnp.float32), unroll=4)
        f_own[ch // 4, pl.ds(ch % 4, 1), :] = jnp.sum(total, axis=0, keepdims=True)

    def f1_copy(d):
        other = (row + d) % ROWS
        return small(f_own.at[other], f_one.at[row], f1_send.at[d], f1_recv.at[row], col_mate(d))

    def f1_wait(d):
        other = (row + d) % ROWS
        small(f_own.at[row], f_one.at[other], f1_send.at[d], f1_recv.at[other], col_mate(d)).wait_recv()

    def f2_copy(d):
        return small(f_sum, f_two.at[me], f2_send.at[d], f2_recv.at[me], row_mate(d))

    def f2_wait(d):
        other = (me + d) % TILES
        small(f_sum, f_two.at[other], f2_send.at[d], f2_recv.at[other], row_mate(d)).wait_recv()

    def f3_copy(d):
        return small(f_all, f_three.at[row], f3_send.at[d], f3_recv.at[row], col_mate(d))

    def f3_wait(d):
        other = (row + d) % ROWS
        small(f_all, f_three.at[other], f3_send.at[d], f3_recv.at[other], col_mate(d)).wait_recv()

    line8 = lax.broadcasted_iota(jnp.int32, (8, 128), 0)

    def field_first():
        f_one[row] = f_own[row]
        loop(1, ROWS, lambda d: f1_copy(d).start())

    def field_second():
        loop(1, ROWS, f1_wait)
        total = f_one[0]
        for r in range(1, ROWS):
            total = total + f_one[r]
        count = jnp.broadcast_to(hdr_ref[...], (8, 128)).astype(jnp.float32)
        total = jnp.where(line8 < 4, total, count)
        f_sum[...] = total
        f_two[me] = total
        loop(1, TILES, lambda d: f2_copy(d).start())

    def field_third():
        loop(1, TILES, f2_wait)
        total = f_two[0]
        for c in range(1, TILES):
            total = total + f_two[c]
        most = jnp.zeros((8, 128), jnp.float32)
        for c in range(TILES):
            most = jnp.maximum(most, f_two[c] + cap // 2)
            if c % 4 < 2:
                most = jnp.maximum(most, f_two[c] + f_two[c + 2])
        total = jnp.where(line8 < 4, total, most)
        f_all[...] = total
        f_three[row] = total
        loop(1, ROWS, lambda d: f3_copy(d).start())

    def field_last():
        loop(1, ROWS, f3_wait)
        most = f_three[0]
        for r in range(1, ROWS):
            most = jnp.maximum(most, f_three[r])
        flag_ref[0, 0] = jnp.max(jnp.where(lane1 == 127, most[4:5, :], 0.0)).astype(jnp.int32)
        for c in range(4):
            line = f_three[row, c : c + 1, :]
            fi_col[c * 128 : (c + 1) * 128, :] = jnp.transpose(jnp.broadcast_to(line, (128, 128)))
        loop(1, ROWS, lambda d: f1_copy(d).wait_send())
        loop(1, TILES, lambda d: f2_copy(d).wait_send())
        loop(1, ROWS, lambda d: f3_copy(d).wait_send())
        loop(1, TILES, lambda d: hr_copy(d).wait_send())
        loop(1, ROWS, lambda d: hc_copy(d).wait_send())


    def one_step(step, carry):
        p = 2 * step
        first = step == 0

        def chips_open(q, from_, to_):
            def one(j):
                for h in range(2):
                    row_in(q, peer_tile(j), h)
                unpack_chip(q % 2, chip_tile(j))

            loop(from_, to_, one)

        def cols_open(from_, to_):
            def one(j):
                tile = col_tile(j)
                small(
                    xbuf.at[step, tile], xbuf.at[step, tile], x_send.at[0], x_recv.at[step, tile], sibling
                ).wait_recv()
                unpack_col(step, tile)

            loop(from_, to_, one)

        def once(*acts):
            @pl.when(first)
            def _():
                for act in acts:
                    act()

        def chunks(from_, to_):
            return lambda: loop(from_, to_, field_chunk)

        over_copy(0).start()
        row_pass(p, (0, 0))
        col_pass(step, (0, 0))
        compact_second(cur, 0, keep_iterate(step))
        row_pass(p, (0, 1))
        col_pass(step, (0, 1))
        once(spread_sites, chunks(0, 9), read_tables)
        chips_open(p, 0, 1)
        cols_open(0, 1)
        col_pass(step, (2, 0), (3, 0))
        row_pass(p, (2, 0), (3, 0), (1, 0))
        across_copy(p, step, 0).start()
        once(chunks(9, 18))
        row_pass(p, (3, 1), (1, 1))
        across_copy(p, step, 1).start()
        col_pass(step, (3, 1), (2, 1))
        row_pass(p, (2, 1))
        once(chunks(18, 26))
        chips_open(p, 1, 3)
        col_pass(step, (1, 0))
        row_pass(p, (6, 0))
        col_pass(step, (1, 1))
        once(chunks(26, 32), field_first)
        chips_open(p, 3, 4)
        row_pass(p, (4, 0), (6, 1), (4, 1))
        cols_open(1, 4)
        row_pass(p, (5, 1), (5, 0))
        col_pass(step, (4, 0), (5, 0), (5, 1), (4, 1))
        once(field_second)
        chips_open(p, 4, 7)
        row_pass(p, (7, 0), (7, 1))
        col_pass(step, (6, 0), (6, 1))
        cols_open(4, 7)
        once(field_third)
        acc[...] = jnp.zeros_like(acc)
        last_z, last_col = chip_tile(7) // 4, col_tile(7)

        def early(r):
            @pl.when((r // 2 != last_z) & (r != last_col))
            def _():
                fold(2 * r, 2 * r + 1)

        loop(0, ROWS, early)
        chips_open(p, 7, 8)
        col_pass(step, (7, 0), (7, 1))

        def late(i):
            r = 2 * last_z + i

            @pl.when(r != last_col)
            def _():
                fold(2 * r, 2 * r + 1)

        loop(0, 2, late)
        cols_open(7, 8)
        fold(2 * last_col, 2 * last_col + 1)
        once(field_last)

        scale = jnp.where(first, 1.0, 0.0)

        def pieces(b):
            at = (pl.ds((b // 2) * BLOCK, BLOCK), pl.ds((b % 2) * 128, 128))
            fi = scale * fi_col[pl.ds((b // 2) * BLOCK, BLOCK), :]
            fj = scale * f_three[me // 2, pl.ds((me % 2) * 2 + b % 2, 1), :]
            same = (sub + (512 * row + (b // 2) * BLOCK)) == (lane + (256 * me + (b % 2) * 128))
            return at, fi, fj, same

        for b in range(16):
            at, fi, fj, same = pieces(b)
            value = acc[at] + (fi + fj) * cur[b] + jnp.where(same, fi * fi, 0.0)
            put(sq, b, value)

        def store(u, value):
            rbuf[1, me, u] = value

        spill(sq, 1)
        over_copy(1).start()
        compact_first(sq, store)
        row_drain(p)
        for h in range(2):
            across_copy(p, step, h).wait_send()

        def chips_fold(from_, to_):
            def one(j):
                for h in range(2):
                    row_in(p + 1, peer_tile(j), h)
                tile = chip_tile(j)
                unpack_chip(1, tile)
                fold(tile, tile + 2)

            loop(from_, to_, one)

        row_pass(p + 1, (0, 0))
        compact_second(sq, 1, store)
        row_pass(p + 1, (0, 1))
        acc[...] = jnp.zeros_like(acc)
        chips_fold(0, 1)
        row_pass(p + 1, (2, 0), (3, 0), (1, 0))
        row_pass(p + 1, (3, 1), (1, 1), (2, 1))
        chips_fold(1, 4)
        row_pass(p + 1, (6, 0), (4, 0), (6, 1))
        row_pass(p + 1, (4, 1), (5, 1), (5, 0))
        chips_fold(4, 7)
        row_pass(p + 1, (7, 1), (7, 0))
        chips_fold(7, 8)

        for b in range(16):
            at, fi, fj, same = pieces(b)
            value = 1.5 * (cur[b] + jnp.where(same, fi, 0.0)) - 0.5 * (acc[at] + sq[b] * fj)
            put(cur, b, value)

        row_drain(p + 1)
        col_drain(step)

        @pl.when(step + 1 < STEPS)
        def _():
            spill(cur, 0)
            compact_first(cur, keep_iterate(step + 1))


        return carry

    lax.fori_loop(0, STEPS, one_step, 0)

    for b in range(16):
        at = (pl.ds((b // 2) * BLOCK, BLOCK), pl.ds((b % 2) * 128, 128))
        keep_left = keep_ref[b // 2, 2 * (b % 2)].astype(jnp.float32)
        keep_right = keep_ref[b // 2, 2 * (b % 2) + 1].astype(jnp.float32)
        out_ref[at] = cur[b] * jnp.where(left, keep_left, keep_right)


def run(cap, number, *operands):
    pairs = cap // 2
    vmem = pl.BlockSpec(memory_space=pltpu.VMEM)
    smem = pl.BlockSpec(memory_space=pltpu.SMEM)
    f32, bf16 = jnp.float32, jnp.bfloat16
    dma = pltpu.SemaphoreType.DMA
    return pl.pallas_call(
        functools.partial(kernel, cap),
        out_shape=(
            jax.ShapeDtypeStruct((512, 256), f32),
            jax.ShapeDtypeStruct((1, 1), jnp.int32),
        ),
        in_specs=[smem, smem, smem, vmem, vmem, vmem, vmem],
        out_specs=(vmem, smem),
        scratch_shapes=[
            pltpu.VMEM((2, TILES, pairs, BLOCK, 128), f32),
            pltpu.VMEM((2, ROWS, pairs, BLOCK, 128), f32),
            pltpu.VMEM((2, ROWS, pairs // 2, BLOCK, 128), f32),
            pltpu.VMEM((2, pairs // 2, BLOCK, 128), f32),
            pltpu.VMEM((2, pairs // 2, BLOCK, 128), f32),
            pltpu.VMEM((TILES, 512, 256), bf16),
            pltpu.VMEM((TILES, 512, 256), bf16),
            pltpu.VMEM((TILES, 256, 256), bf16),
            pltpu.VMEM((TILES, 256, 256), bf16),
            pltpu.VMEM((512, 256), f32),
            pltpu.VMEM((4 * pairs + 2, BLOCK, 128), f32),
            pltpu.VMEM((32, BLOCK, 128), f32),
            pltpu.VMEM((32, BLOCK, 128), f32),
            pltpu.VMEM((4, 512, 128), f32),
            pltpu.VMEM((ROWS, 8, 128), f32),
            pltpu.VMEM((ROWS, 8, 128), f32),
            pltpu.VMEM((TILES, 8, 128), f32),
            pltpu.VMEM((ROWS, 8, 128), f32),
            pltpu.VMEM((8, 128), f32),
            pltpu.VMEM((8, 128), f32),
            pltpu.VMEM((512, 128), f32),
            pltpu.VMEM((1, 128), jnp.int32),
            pltpu.VMEM((1, 128), jnp.int32),
            pltpu.VMEM((1, 128), f32),
            pltpu.VMEM((TILES, 1, 128), jnp.int32),
            pltpu.VMEM((ROWS, 1, 128), jnp.int32),
            pltpu.SMEM((1, 128), jnp.int32),
            pltpu.SMEM((1, 128), f32),
            pltpu.SMEM((TILES, 1, 128), jnp.int32),
            pltpu.SMEM((ROWS, 1, 128), jnp.int32),
            dma((8, 4, 2)),
            dma((4, TILES, 2)),
            dma((8, 3, 2)),
            dma((2, ROWS, 2)),
            dma((ROWS,)),
            dma((2, ROWS)),
            dma((2,)),
            dma((2,)),
            dma((TILES,)),
            dma((TILES,)),
            dma((ROWS,)),
            dma((ROWS,)),
            dma((ROWS,)),
            dma((ROWS,)),
            dma((TILES,)),
            dma((TILES,)),
            dma((ROWS,)),
            dma((ROWS,)),
            dma((2,)),
        ],
        compiler_params=pltpu.CompilerParams(
            collective_id=number, has_side_effects=True, vmem_limit_bytes=58 * 1024 * 1024
        ),
    )(*operands)


def body(centers, charge_sites, charges, amplitudes, widths, core_matrix, pattern):
    operands = (
        pattern,
        amplitudes,
        widths,
        centers,
        charge_sites,
        charges[None, :],
        core_matrix,
    )
    out, flag = run(CAP, 0, *operands)
    return lax.cond(flag[0, 0] > 2 * CAP, lambda: run(FULL, 1, *operands)[0], lambda: out)


def solution(mesh):
    return jax.shard_map(
        body,
        mesh=mesh,
        in_specs=(
            P(),
            P(None, AXES),
            P(AXES),
            P(),
            P(),
            P("row", ("col", "sec")),
            P("row", ("col", "sec")),
        ),
        out_specs=P("row", ("col", "sec")),
        check_vma=False,
    )
```

```python
import functools

import jax
import jax.numpy as jnp
from jax import lax
from jax.experimental import pallas as pl
from jax.experimental.pallas import tpu as pltpu
from jax.sharding import PartitionSpec as P

BLOCK = 64
STEPS = 2
ROWS, COLS, SECS = 8, 8, 2
TILES = COLS * SECS
CAP = 16
FULL = 32
CHUNK = 128
LOG2E = 1.4426950408889634
MESH = pl.DeviceIdType.MESH
AXES = ("row", "col", "sec")


def kernel(
    cap,
    keep_ref,
    amp_ref,
    width_ref,
    centers_ref,
    sites_ref,
    charges_ref,
    core_ref,
    out_ref,
    flag_ref,
    rbuf,
    cbuf,
    xbuf,
    over_out,
    over_in,
    a_hi,
    a_lo,
    b_hi,
    b_lo,
    acc,
    work,
    cur,
    sq,
    fan,
    f_own,
    f_one,
    f_two,
    f_three,
    f_sum,
    f_all,
    fi_col,
    hdr_ref,
    inv_line,
    coef_line,
    hrow,
    hcol,
    inv_ref,
    coef_ref,
    trow,
    tcol,
    r_send,
    r_recv,
    c_send,
    c_recv,
    x_send,
    x_recv,
    o_send,
    o_recv,
    hr_send,
    hr_recv,
    hc_send,
    hc_recv,
    f1_send,
    f1_recv,
    f2_send,
    f2_recv,
    f3_send,
    f3_recv,
    t_sem,
):
    pairs = cap // 2
    half = pairs // 2
    row, col, sec = lax.axis_index("row"), lax.axis_index("col"), lax.axis_index("sec")
    hi, y = row // 4, row % 4
    z, core = col // 2, col % 2
    me = 2 * col + sec

    sibling = (row, 2 * z + (1 - core), sec)
    x_peer = (row, col, 1 - sec)
    z_up = (row, 2 * ((z + 1) % 4) + core, sec)
    z_down = (row, 2 * ((z + 3) % 4) + core, sec)
    across = ((row + 4) % 8, col, 1 - sec)
    y_up = (4 * hi + (y + 1) % 4, col, sec)
    y_down = (4 * hi + (y + 3) % 4, col, sec)

    def row_mate(d):
        other = (me + d) % TILES
        return (row, other // 2, other % 2)

    def col_mate(d):
        return ((row + d) % ROWS, col, sec)

    lane = lax.broadcasted_iota(jnp.int32, (BLOCK, 128), 1)
    sub = lax.broadcasted_iota(jnp.int32, (BLOCK, 128), 0)
    left = lane < BLOCK

    barrier = pltpu.get_barrier_semaphore()

    def greet_row(d, c):
        pl.semaphore_signal(barrier, inc=1, device_id=row_mate(d), device_id_type=MESH)
        return c

    def greet_col(d, c):
        pl.semaphore_signal(barrier, inc=1, device_id=col_mate(d), device_id_type=MESH)
        return c

    lax.fori_loop(1, TILES, greet_row, 0)
    lax.fori_loop(1, ROWS, greet_col, 0)
    pl.semaphore_signal(barrier, inc=1, device_id=across, device_id_type=MESH)


    lane1 = lax.broadcasted_iota(jnp.int32, (1, 128), 1)
    before = 0
    empty = 2 * pairs
    codes = jnp.full((1, 128), empty, jnp.int32)
    blocks = jnp.zeros((1, 128), jnp.int32)
    for b in range(32):
        keep = keep_ref[b // 4, b % 4]
        turned = (before + b) % 2
        spare = 2 * cap - 1 - before
        own = core * pairs + before // 2 + (2 * pairs + 1) * turned
        other = (1 - core) * pairs + spare // 2 + (2 * pairs + 1) * (1 - turned)
        code = jnp.where(before < cap, own, jnp.where(spare >= cap // 2, other, empty))
        code = jnp.where(keep == 1, code, empty)
        codes = jnp.where(lane1 == b, code, codes)
        at = jnp.where(before < cap, before, jnp.where(spare >= cap // 2, 64 + spare, 127))
        at = jnp.where(keep == 1, at, 127)
        blocks = jnp.where(lane1 == at, b // 2 + 16 * ((at + b) % 2), blocks)
        before = before + keep
    hdr_ref[...] = jnp.where(lane1 == 127, before, codes)
    inv_line[...] = jnp.where(lane1 < 127, blocks, 0)
    scale_line = jnp.zeros((1, 128), jnp.float32)
    for g in range(6):
        wide = jnp.full((1, 128), width_ref[g], jnp.float32)
        scale_line = jnp.where(lane1 == g, -LOG2E / (wide * wide), scale_line)
    coef_line[...] = scale_line
    inv_copy = pltpu.make_async_copy(inv_line, inv_ref, t_sem.at[0])
    coef_copy = pltpu.make_async_copy(coef_line, coef_ref, t_sem.at[1])
    inv_copy.start()
    coef_copy.start()


    def put(dst, number, value):
        dst[number] = value
        dst[16 + number] = pltpu.roll(value, BLOCK, 1)

    def pair(src, first_slot):
        return jnp.where(left, src[inv_ref[0, first_slot]], src[inv_ref[0, first_slot + 1]])

    def over_copy(q):
        return pltpu.make_async_remote_copy(
            src_ref=over_out.at[q],
            dst_ref=over_in.at[q],
            send_sem=o_send.at[q],
            recv_sem=o_recv.at[q],
            device_id=sibling,
            device_id_type=MESH,
        )

    def spill(src, q):
        for u in range(half):
            over_out[q, u] = pair(src, 64 + 2 * (half + u))

    def compact_first(src, store):
        for u in range(half):
            store(u, pair(src, 2 * u))

    def compact_second(src, q, store):
        over_copy(q).wait()
        for u in range(half, pairs):
            slot = 2 * u + jnp.where(left, 0, 1)
            store(u, jnp.where(slot < before, pair(src, 2 * u), over_in[q, u - half]))

    def lay(number, value):
        work[number] = value
        work[2 * pairs + 1 + number] = pltpu.roll(value, BLOCK, 1)

    def unpack(table, tile, store):
        for b in range(16):
            value = jnp.where(
                left, work[table[tile, 0, 2 * b]], work[table[tile, 0, 2 * b + 1]]
            )
            high = value.astype(jnp.bfloat16)
            low = (value - high.astype(jnp.float32)).astype(jnp.bfloat16)
            store(b, high, low)

    def unpack_chip(q, tile):
        for u in range(pairs):
            lay(u, rbuf[q, tile, u])
            lay(pairs + u, rbuf[q, tile + 2, u])

        def one(i, c):
            at_tile = tile + 2 * i

            def store(b, high, low):
                at = (at_tile, pl.ds((b // 2) * BLOCK, BLOCK), pl.ds((b % 2) * 128, 128))
                a_hi[at] = high
                a_lo[at] = low

            unpack(trow, at_tile, store)
            return c

        lax.fori_loop(0, 2, one, 0)

    def unpack_col(s, tile):
        for u in range(pairs):
            lay(core * pairs + u, cbuf[s, tile, u])
        for u in range(half):
            lay((1 - core) * pairs + half + u, xbuf[s, tile, u])

        def store(b, high, low):
            at = (
                2 * tile + b // 8,
                pl.ds((b // 2 % 4) * BLOCK, BLOCK),
                pl.ds((b % 2) * 128, 128),
            )
            b_hi[at] = high
            b_lo[at] = low

        unpack(tcol, tile, store)

    def fold(*tiles):
        dot = functools.partial(jnp.dot, preferred_element_type=jnp.float32)
        total = acc[...]
        for tile in tiles:
            total = total + dot(a_hi[tile], b_hi[tile])
            total = total + dot(a_lo[tile], b_hi[tile])
            total = total + dot(a_hi[tile], b_lo[tile])
        acc[...] = total


    def row_copy(p, tile, j, kind, h, dev):
        ref = rbuf.at[p % 2, tile, pl.ds(h * half, half)]
        return pltpu.make_async_remote_copy(
            src_ref=ref,
            dst_ref=ref,
            send_sem=r_send.at[j, kind, h],
            recv_sem=r_recv.at[p, tile, h],
            device_id=dev,
            device_id_type=MESH,
        )

    def col_copy(s, tile, j, kind, h, dev):
        ref = cbuf.at[s, tile, pl.ds(h * half, half)]
        return pltpu.make_async_remote_copy(
            src_ref=ref,
            dst_ref=ref,
            send_sem=c_send.at[j, kind, h],
            recv_sem=c_recv.at[s, tile, h],
            device_id=dev,
            device_id_type=MESH,
        )


    def mid(j):
        return (j + 2) // 4 % 2

    def hop(j):
        return mid(j) * (3 - 2 * (j % 2)) + (1 - mid(j)) * 2 * (j // 6)

    def swap(j):
        return mid(j) * (j // 2 - 1) + (1 - mid(j)) * (j % 2)

    def chip_tile(j):
        return 4 * ((z + hop(j)) % 4) + (sec + swap(j)) % 2

    def row_tile(j):
        return chip_tile(j) + 2 * core

    def peer_tile(j):
        return chip_tile(j) + 2 * (1 - core)

    def col_tile(j):
        return 4 * ((hi + swap(j)) % 2) + (y + hop(j)) % 4

    def across_copy(p, s, h):
        piece = pl.ds(h * half, half)
        return pltpu.make_async_remote_copy(
            src_ref=rbuf.at[p % 2, row_tile(1), piece],
            dst_ref=cbuf.at[s, row, piece],
            send_sem=c_send.at[0, 2, h],
            recv_sem=c_recv.at[s, row, h],
            device_id=across,
            device_id_type=MESH,
        )

    def x_copy(s, j):
        tile = col_tile(j)
        return pltpu.make_async_remote_copy(
            src_ref=cbuf.at[s, tile, pl.ds(half, half)],
            dst_ref=xbuf.at[s, tile],
            send_sem=x_send.at[j],
            recv_sem=x_recv.at[s, tile],
            device_id=sibling,
            device_id_type=MESH,
        )

    row_plan = {
        (0, 0): (1, 2, 3, 0),
        (0, 1): (1, 2, 3, 0),
        (1, 0): (0,),
        (1, 1): (1, 2, 0),
        (2, 0): (1, 3, 0),
        (2, 1): (0,),
        (3, 0): (3, 0),
        (3, 1): (2, 0),
        (4, 0): (0,),
        (4, 1): (1, 0),
        (5, 0): (0,),
        (5, 1): (2, 0),
        (6, 0): (3, 0),
        (6, 1): (0,),
        (7, 0): (0,),
        (7, 1): (0,),
    }
    col_plan = {
        (0, 0): (0, 1),
        (0, 1): (0, 1),
        (1, 0): (0, 1),
        (1, 1): (0, 1),
        (2, 0): (0,),
        (2, 1): (),
        (3, 0): (),
        (3, 1): (1,),
        (4, 0): (0,),
        (4, 1): (),
        (5, 0): (),
        (5, 1): (1,),
        (6, 0): (),
        (6, 1): (),
        (7, 0): (),
        (7, 1): (),
    }
    row_to = (sibling, z_up, z_down, x_peer)
    col_to = (y_up, y_down)

    def row_act(p, j, h, kind, act):
        def go():
            act(row_copy(p, row_tile(j), j, kind, h, row_to[kind]))

        if j in (4, 5) and kind > 0:
            pl.when(core == j - 4)(go)
        else:
            go()

    def col_act(s, j, h, kind, act):
        act(col_copy(s, col_tile(j), j, kind, h, col_to[kind]))

    def start(copy):
        copy.start()

    def row_pass(p, *pieces):
        for j, h in pieces:
            if j > 0:
                row_in(p, row_tile(j), h)
            for kind in row_plan[j, h]:
                row_act(p, j, h, kind, start)

    def col_pass(s, *pieces):
        for j, h in pieces:
            if j > 0:
                col_in(s, col_tile(j), h)
            for kind in col_plan[j, h]:
                col_act(s, j, h, kind, start)
            if h == 1:
                x_copy(s, j).start()

    def drain(copy):
        copy.wait_send()

    def row_in(p, tile, h):
        row_copy(p, tile, 0, 0, h, sibling).wait_recv()

    def col_in(s, tile, h):
        col_copy(s, tile, 0, 0, h, y_up).wait_recv()

    def row_drain(p):
        for (j, h), kinds in row_plan.items():
            for kind in kinds:
                row_act(p, j, h, kind, drain)

    def col_drain(s):
        for (j, h), kinds in col_plan.items():
            for kind in kinds:
                col_act(s, j, h, kind, drain)
            if h == 1:
                x_copy(s, j).wait_send()

    def small(src, dst, send, recv, dev):
        return pltpu.make_async_remote_copy(
            src_ref=src, dst_ref=dst, send_sem=send, recv_sem=recv,
            device_id=dev, device_id_type=MESH,
        )

    def loop(first, last, f):
        def one(d, c):
            f(d)
            return c

        lax.fori_loop(first, last, one, 0)


    for b in range(16):
        put(cur, b, core_ref[pl.ds((b // 2) * BLOCK, BLOCK), pl.ds((b % 2) * 128, 128)])

    def keep_iterate(s):
        def store(u, value):
            rbuf[0, me, u] = value
            cbuf[s, row, u] = value

        return store

    inv_copy.wait()
    coef_copy.wait()
    spill(cur, 0)
    compact_first(cur, keep_iterate(0))
    work[empty] = jnp.zeros((BLOCK, 128), jnp.float32)
    work[4 * pairs + 1] = jnp.zeros((BLOCK, 128), jnp.float32)
    hrow[me] = hdr_ref[...]
    hcol[row] = hdr_ref[...]

    def f1_copy(d):
        return small(f_one.at[row], f_one.at[row], f1_send.at[d], f1_recv.at[row], col_mate(d))

    def hr_copy(d):
        return small(hdr_ref, hrow.at[me], hr_send.at[d], hr_recv.at[me], row_mate(d))

    def hc_copy(d):
        return small(hdr_ref, hcol.at[row], hc_send.at[d], hc_recv.at[row], col_mate(d))

    for c in range(4):
        for a in range(3):
            f_one[row, 4 * a + c : 4 * a + c + 1, :] = sites_ref[a : a + 1, c * 128 : (c + 1) * 128]
        f_one[row, 12 + c : 13 + c, :] = charges_ref[0:1, c * 128 : (c + 1) * 128]
    pl.semaphore_wait(barrier, TILES + ROWS - 1)
    loop(1, ROWS, lambda d: f1_copy(d).start())
    loop(1, TILES, lambda d: hr_copy(d).start())
    loop(1, ROWS, lambda d: hc_copy(d).start())

    def read_tables():
        def wait_row(d):
            other = (me + d) % TILES
            small(hdr_ref, hrow.at[other], hr_send.at[d], hr_recv.at[other], row_mate(d)).wait_recv()

        def wait_col(d):
            other = (row + d) % ROWS
            small(hdr_ref, hcol.at[other], hc_send.at[d], hc_recv.at[other], col_mate(d)).wait_recv()

        loop(1, TILES, wait_row)
        loop(1, ROWS, wait_col)
        one = pltpu.make_async_copy(hrow, trow, t_sem.at[0])
        two = pltpu.make_async_copy(hcol, tcol, t_sem.at[1])
        one.start()
        two.start()
        one.wait()
        two.wait()


    def spread_centers():
        for a in range(3):
            for c in range(4):
                at = pl.ds(pl.multiple_of(row * 512 + c * 128, 128), 128)
                fan[a, c * 128 : (c + 1) * 128, :] = jnp.transpose(
                    jnp.broadcast_to(centers_ref[a : a + 1, at], (128, 128))
                )
        f_own[...] = jnp.zeros_like(f_own)

    def field_chunk(ch):
        mate, c = (row + ch // 4) % ROWS, ch % 4
        px = f_one[mate, pl.ds(c, 1), :]
        py = f_one[mate, pl.ds(4 + c, 1), :]
        pz = f_one[mate, pl.ds(8 + c, 1), :]
        charge = f_one[mate, pl.ds(12 + c, 1), :]

        def some(m, carry):
            part = pl.ds(m * 32, 32)
            dx = fan[0, part, :] - px
            dy = fan[1, part, :] - py
            dz = fan[2, part, :] - pz
            distance = dx * dx + dy * dy + dz * dz
            value = amp_ref[0] * jnp.exp2(distance * coef_ref[0, 0])
            for g in range(1, 6):
                value = value + amp_ref[g] * jnp.exp2(distance * coef_ref[0, g])
            f_own[part, :] += value * charge
            return carry

        lax.fori_loop(0, 16, some, 0, unroll=4)

    def f1_wait(d):
        other = (row + d) % ROWS
        small(f_one.at[other], f_one.at[other], f1_send.at[d], f1_recv.at[other], col_mate(d)).wait_recv()

    def f2_copy(d):
        return small(f_sum, f_two.at[me], f2_send.at[d], f2_recv.at[me], row_mate(d))

    def f2_wait(d):
        other = (me + d) % TILES
        small(f_sum, f_two.at[other], f2_send.at[d], f2_recv.at[other], row_mate(d)).wait_recv()

    def f3_copy(d):
        return small(f_all, f_three.at[row], f3_send.at[d], f3_recv.at[row], col_mate(d))

    def f3_wait(d):
        other = (row + d) % ROWS
        small(f_all, f_three.at[other], f3_send.at[d], f3_recv.at[other], col_mate(d)).wait_recv()

    line8 = lax.broadcasted_iota(jnp.int32, (8, 128), 0)

    def charges_in():
        loop(1, ROWS, f1_wait)

    def field_second():
        lines = [
            jnp.sum(jnp.transpose(f_own[c * 128 : (c + 1) * 128, :]), axis=0, keepdims=True)
            for c in range(4)
        ]
        total = jnp.concatenate(lines + lines, axis=0)
        count = jnp.broadcast_to(hdr_ref[...], (8, 128)).astype(jnp.float32)
        total = jnp.where(line8 < 4, total, count)
        f_sum[...] = total
        f_two[me] = total
        loop(1, TILES, lambda d: f2_copy(d).start())

    def field_third():
        loop(1, TILES, f2_wait)
        total = f_two[0]
        for c in range(1, TILES):
            total = total + f_two[c]
        most = jnp.zeros((8, 128), jnp.float32)
        for c in range(TILES):
            most = jnp.maximum(most, f_two[c] + cap // 2)
            if c % 4 < 2:
                most = jnp.maximum(most, f_two[c] + f_two[c + 2])
        total = jnp.where(line8 < 4, total, most)
        f_all[...] = total
        f_three[row] = total
        loop(1, ROWS, lambda d: f3_copy(d).start())

    def field_last():
        loop(1, ROWS, f3_wait)
        most = f_three[0]
        for r in range(1, ROWS):
            most = jnp.maximum(most, f_three[r])
        flag_ref[0, 0] = jnp.max(jnp.where(lane1 == 127, most[4:5, :], 0.0)).astype(jnp.int32)
        for c in range(4):
            line = f_three[row, c : c + 1, :]
            fi_col[c * 128 : (c + 1) * 128, :] = jnp.transpose(jnp.broadcast_to(line, (128, 128)))
        loop(1, ROWS, lambda d: f1_copy(d).wait_send())
        loop(1, TILES, lambda d: f2_copy(d).wait_send())
        loop(1, ROWS, lambda d: f3_copy(d).wait_send())
        loop(1, TILES, lambda d: hr_copy(d).wait_send())
        loop(1, ROWS, lambda d: hc_copy(d).wait_send())


    def one_step(step, carry):
        p = 2 * step
        first = step == 0

        def chips_open(q, from_, to_):
            def one(j):
                for h in range(2):
                    row_in(q, peer_tile(j), h)
                unpack_chip(q % 2, chip_tile(j))

            loop(from_, to_, one)

        def cols_open(from_, to_):
            def one(j):
                tile = col_tile(j)
                small(
                    xbuf.at[step, tile], xbuf.at[step, tile], x_send.at[0], x_recv.at[step, tile], sibling
                ).wait_recv()
                unpack_col(step, tile)

            loop(from_, to_, one)

        def once(*acts):
            @pl.when(first)
            def _():
                for act in acts:
                    act()

        def chunks(from_, to_):
            return lambda: loop(from_, to_, field_chunk)

        over_copy(0).start()
        row_pass(p, (0, 0))
        col_pass(step, (0, 0))
        compact_second(cur, 0, keep_iterate(step))
        row_pass(p, (0, 1))
        col_pass(step, (0, 1))
        acc[...] = jnp.zeros_like(acc)
        once(spread_centers, chunks(0, 4), charges_in, chunks(4, 8))
        row_pass(p, (1, 0))
        across_copy(p, step, 0).start()
        col_pass(step, (2, 0))
        row_pass(p, (2, 0), (3, 0))
        once(read_tables, chunks(8, 12))
        chips_open(p, 0, 1)
        row_pass(p, (1, 1))
        across_copy(p, step, 1).start()
        col_pass(step, (3, 1))
        row_pass(p, (3, 1), (2, 1))
        col_pass(step, (2, 1), (3, 0))
        once(chunks(12, 15))
        col_pass(step, (1, 0))
        cols_open(0, 1)
        once(chunks(15, 20))
        chips_open(p, 1, 2)
        row_pass(p, (6, 0))
        col_pass(step, (1, 1))
        once(chunks(20, 26))
        row_pass(p, (4, 1), (5, 1), (6, 1), (4, 0), (5, 0))
        col_pass(step, (4, 0))
        once(chunks(26, 32), field_second)
        chips_open(p, 2, 4)
        cols_open(1, 4)
        col_pass(step, (5, 0), (5, 1), (4, 1))
        chips_open(p, 4, 6)
        once(field_third)
        row_pass(p, (7, 1), (7, 0))
        chips_open(p, 6, 7)
        col_pass(step, (6, 0), (6, 1))
        cols_open(4, 7)
        acc[...] = jnp.zeros_like(acc)
        last_z, last_col = chip_tile(7) // 4, col_tile(7)

        def early(r):
            @pl.when((r // 2 != last_z) & (r != last_col))
            def _():
                fold(2 * r, 2 * r + 1)

        loop(0, ROWS, early)
        chips_open(p, 7, 8)
        col_pass(step, (7, 0), (7, 1))

        def late(i):
            r = 2 * last_z + i

            @pl.when(r != last_col)
            def _():
                fold(2 * r, 2 * r + 1)

        loop(0, 2, late)
        cols_open(7, 8)
        fold(2 * last_col, 2 * last_col + 1)
        once(field_last)

        scale = jnp.where(first, 1.0, 0.0)

        def pieces(b):
            at = (pl.ds((b // 2) * BLOCK, BLOCK), pl.ds((b % 2) * 128, 128))
            fi = scale * fi_col[pl.ds((b // 2) * BLOCK, BLOCK), :]
            fj = scale * f_three[me // 2, pl.ds((me % 2) * 2 + b % 2, 1), :]
            same = (sub + (512 * row + (b // 2) * BLOCK)) == (lane + (256 * me + (b % 2) * 128))
            return at, fi, fj, same

        for b in range(16):
            at, fi, fj, same = pieces(b)
            value = acc[at] + (fi + fj) * cur[b] + jnp.where(same, fi * fi, 0.0)
            put(sq, b, value)

        def store(u, value):
            rbuf[1, me, u] = value

        spill(sq, 1)
        over_copy(1).start()
        compact_first(sq, store)
        row_drain(p)
        for h in range(2):
            across_copy(p, step, h).wait_send()

        def chips_fold(from_, to_):
            def one(j):
                for h in range(2):
                    row_in(p + 1, peer_tile(j), h)
                tile = chip_tile(j)
                unpack_chip(1, tile)
                fold(tile, tile + 2)

            loop(from_, to_, one)

        row_pass(p + 1, (0, 0))
        compact_second(sq, 1, store)
        row_pass(p + 1, (0, 1))
        acc[...] = jnp.zeros_like(acc)
        row_pass(p + 1, (2, 0), (3, 0), (1, 0))
        chips_fold(0, 1)
        row_pass(p + 1, (1, 1), (3, 1), (2, 1))
        chips_fold(1, 2)
        row_pass(p + 1, (6, 0))
        chips_fold(2, 3)
        row_pass(p + 1, (4, 1), (5, 1), (6, 1), (4, 0), (5, 0))
        chips_fold(3, 5)
        row_pass(p + 1, (7, 1), (7, 0))
        chips_fold(5, 7)
        chips_fold(7, 8)

        for b in range(16):
            at, fi, fj, same = pieces(b)
            value = 1.5 * (cur[b] + jnp.where(same, fi, 0.0)) - 0.5 * (acc[at] + sq[b] * fj)
            put(cur, b, value)

        row_drain(p + 1)
        col_drain(step)

        @pl.when(step + 1 < STEPS)
        def _():
            spill(cur, 0)
            compact_first(cur, keep_iterate(step + 1))


        return carry

    lax.fori_loop(0, STEPS, one_step, 0)

    for b in range(16):
        at = (pl.ds((b // 2) * BLOCK, BLOCK), pl.ds((b % 2) * 128, 128))
        keep_left = keep_ref[b // 2, 2 * (b % 2)].astype(jnp.float32)
        keep_right = keep_ref[b // 2, 2 * (b % 2) + 1].astype(jnp.float32)
        out_ref[at] = cur[b] * jnp.where(left, keep_left, keep_right)


def run(cap, number, *operands):
    pairs = cap // 2
    vmem = pl.BlockSpec(memory_space=pltpu.VMEM)
    smem = pl.BlockSpec(memory_space=pltpu.SMEM)
    f32, bf16 = jnp.float32, jnp.bfloat16
    dma = pltpu.SemaphoreType.DMA
    return pl.pallas_call(
        functools.partial(kernel, cap),
        out_shape=(
            jax.ShapeDtypeStruct((512, 256), f32),
            jax.ShapeDtypeStruct((1, 1), jnp.int32),
        ),
        in_specs=[smem, smem, smem, vmem, vmem, vmem, vmem],
        out_specs=(vmem, smem),
        scratch_shapes=[
            pltpu.VMEM((2, TILES, pairs, BLOCK, 128), f32),
            pltpu.VMEM((2, ROWS, pairs, BLOCK, 128), f32),
            pltpu.VMEM((2, ROWS, pairs // 2, BLOCK, 128), f32),
            pltpu.VMEM((2, pairs // 2, BLOCK, 128), f32),
            pltpu.VMEM((2, pairs // 2, BLOCK, 128), f32),
            pltpu.VMEM((TILES, 512, 256), bf16),
            pltpu.VMEM((TILES, 512, 256), bf16),
            pltpu.VMEM((TILES, 256, 256), bf16),
            pltpu.VMEM((TILES, 256, 256), bf16),
            pltpu.VMEM((512, 256), f32),
            pltpu.VMEM((4 * pairs + 2, BLOCK, 128), f32),
            pltpu.VMEM((32, BLOCK, 128), f32),
            pltpu.VMEM((32, BLOCK, 128), f32),
            pltpu.VMEM((3, 512, 128), f32),
            pltpu.VMEM((512, 128), f32),
            pltpu.VMEM((ROWS, 16, 128), f32),
            pltpu.VMEM((TILES, 8, 128), f32),
            pltpu.VMEM((ROWS, 8, 128), f32),
            pltpu.VMEM((8, 128), f32),
            pltpu.VMEM((8, 128), f32),
            pltpu.VMEM((512, 128), f32),
            pltpu.VMEM((1, 128), jnp.int32),
            pltpu.VMEM((1, 128), jnp.int32),
            pltpu.VMEM((1, 128), f32),
            pltpu.VMEM((TILES, 1, 128), jnp.int32),
            pltpu.VMEM((ROWS, 1, 128), jnp.int32),
            pltpu.SMEM((1, 128), jnp.int32),
            pltpu.SMEM((1, 128), f32),
            pltpu.SMEM((TILES, 1, 128), jnp.int32),
            pltpu.SMEM((ROWS, 1, 128), jnp.int32),
            dma((8, 4, 2)),
            dma((4, TILES, 2)),
            dma((8, 3, 2)),
            dma((2, ROWS, 2)),
            dma((ROWS,)),
            dma((2, ROWS)),
            dma((2,)),
            dma((2,)),
            dma((TILES,)),
            dma((TILES,)),
            dma((ROWS,)),
            dma((ROWS,)),
            dma((ROWS,)),
            dma((ROWS,)),
            dma((TILES,)),
            dma((TILES,)),
            dma((ROWS,)),
            dma((ROWS,)),
            dma((2,)),
        ],
        compiler_params=pltpu.CompilerParams(
            collective_id=number, has_side_effects=True, vmem_limit_bytes=58 * 1024 * 1024
        ),
    )(*operands)


def body(centers, charge_sites, charges, amplitudes, widths, core_matrix, pattern):
    operands = (
        pattern,
        amplitudes,
        widths,
        centers,
        charge_sites,
        charges[None, :],
        core_matrix,
    )
    out, flag = run(CAP, 0, *operands)
    return lax.cond(flag[0, 0] > 2 * CAP, lambda: run(FULL, 1, *operands)[0], lambda: out)


def solution(mesh):
    return jax.shard_map(
        body,
        mesh=mesh,
        in_specs=(
            P(),
            P(None, AXES),
            P(AXES),
            P(),
            P(),
            P("row", ("col", "sec")),
            P("row", ("col", "sec")),
        ),
        out_specs=P("row", ("col", "sec")),
        check_vma=False,
    )
```
